512 devices in a mesh: gx: 32 (over x, z), gy: 16 (over y, core).
Axes of the slice: x: 4, y: 8, z: 8, core: 2. Of those that a mesh axis runs over, the one named last changes fastest.
Arguments:
- rhs: float32 [512, 512, 128], P('gx', 'gy'), may hold values from -6 to 6
- target: float32 [512, 512, 128], P('gx', 'gy'), may hold values from -6 to 6
- stencils: float32 [9, 27], replicated, may hold values from -0.006 to 0.11, as said below
- face_mask: int32 [6], replicated, may hold values 0 or 1
Outputs:
- solution: float32 [512, 512, 128], P('gx', 'gy')
- grad_rhs: float32 [512, 512, 128], P('gx', 'gy')
- grad_stencils: float32 [9, 27], replicated
The draws below stay inside these ranges and needn't reach their ends.
Inputs may be any that keep to these rules, and one draw needn't show every extreme that they name: `stencils`: entry 13 of every row lies in 0.05 to 0.11, entries 4, 10, 12, 14, 16, 22 in 0.005 to 0.02, the others in -0.006 to 0.006.
All inputs are finite; a program needn't handle non-finite values.
Results may differ from the reference program's by a relative error of at most 0.00002.
Values sent between devices are 32-bit elements; how exact they have to be, the bound alone decides.
A program may use at most 128 MiB of HBM per device.

```python
import jax
import jax.numpy as jnp

NZ = 128
LEVELS = 4
SWEEPS = 3
NX = 512
NY = 512
CELLS = 33554432


def draw_stencils(key, part):
    rows = 2 * LEVELS + 1
    key_center, key_face, key_other = jax.random.split(jax.random.fold_in(key, 17), 3)
    center = jax.random.uniform(key_center, (rows, 27), jnp.float32, 0.06, 0.1)
    facing = jax.random.uniform(key_face, (rows, 27), jnp.float32, 0.005, 0.02)
    others = jax.random.uniform(key_other, (rows, 27), jnp.float32, -0.006, 0.006)
    column = jnp.arange(27)
    is_face = (column == 4) | (column == 10) | (column == 12) | (column == 14) | (column == 16) | (column == 22)
    picked = jnp.where(column == 13, center, jnp.where(is_face, facing, others))
    return picked.astype(jnp.float32)


def touch_ends(values, rng, smallest, high):
    shape = values.shape
    place = [jax.random.randint(jax.random.fold_in(rng, axis), (), 0, shape[axis]) for axis in range(len(shape))]
    values = values.at[tuple(place)].set(smallest)
    longest = shape.index(max(shape))
    place[longest] = (place[longest] + 1) % shape[longest]
    return values.at[tuple(place)].set(high)


def block_levels(key, dims, shards, least, high):
    level, own = 1.0, jax.random.fold_in(key, 6)
    for dim, shards_of in shards:
        steps = jnp.exp(jax.random.uniform(jax.random.fold_in(own, dim), (shards_of,), jnp.float32, least / len(shards), high / len(shards)))
        level = level * jnp.repeat(steps, dims[dim] // shards_of).reshape([-1 if axis == dim else 1 for axis in range(len(dims))])
    return level


def bell_draw(rng, shape, deviation, reach, cuts=(), kind=jnp.bfloat16):
    entries = deviation * jax.random.normal(rng, shape, jnp.float32)
    if cuts:
        entries = entries * block_levels(rng, shape, cuts, -0.22, 0.18)
    return jnp.clip(entries, -reach, reach).astype(kind)


def setup_inputs(seed: int = 0) -> dict:
    arg_keys = jax.random.split(jax.random.key(seed), 5)
    rhs = bell_draw(arg_keys[0], (NX, NY, NZ), 1.0, 6.0, ((0, 32), (1, 16)), jnp.float32)
    target = bell_draw(arg_keys[1], (NX, NY, NZ), 1.0, 6.0, ((0, 32), (1, 16)), jnp.float32)
    stencils = draw_stencils(jax.random.fold_in(arg_keys[4], 71), 0)
    face_mask = touch_ends((jax.random.randint(arg_keys[3], (6,), 0, 2) < 1).astype(jnp.int32), jax.random.fold_in(arg_keys[3], 1), 0, 1)
    return dict(rhs=rhs, target=target, stencils=stencils, face_mask=face_mask)


def shifted_sum(padded, weights, shape):
    total = jnp.zeros(shape, jnp.float32)
    for shift_first in range(3):
        for shift_second in range(3):
            for shift_third in range(3):
                window = padded[shift_first:shift_first + shape[0], shift_second:shift_second + shape[1], shift_third:shift_third + shape[2]]
                total = total + weights[9 * shift_first + 3 * shift_second + shift_third] * window
    return total

def smooth(field, weights):
    return shifted_sum(jnp.pad(field, 1), weights, field.shape)

def face_tally(shape, face_mask):
    walls = face_mask.astype(jnp.float32)
    first = jnp.arange(shape[0])[:, None, None]
    second = jnp.arange(shape[1])[None, :, None]
    third = jnp.arange(shape[2])[None, None, :]
    tally = walls[0] * (first == 0).astype(jnp.float32) + walls[1] * (first == shape[0] - 1).astype(jnp.float32)
    tally = tally + walls[2] * (second == 0).astype(jnp.float32) + walls[3] * (second == shape[1] - 1).astype(jnp.float32)
    tally = tally + walls[4] * (third == 0).astype(jnp.float32) + walls[5] * (third == shape[2] - 1).astype(jnp.float32)
    return tally

def operate(field, tally):
    padded = jnp.pad(field, 1)
    beside = padded[2:, 1:-1, 1:-1] + padded[:-2, 1:-1, 1:-1]
    beside = beside + padded[1:-1, 2:, 1:-1] + padded[1:-1, :-2, 1:-1]
    beside = beside + padded[1:-1, 1:-1, 2:] + padded[1:-1, 1:-1, :-2]
    return (6.0 - tally) * field - beside

def restrict(field):
    shape = field.shape
    return field.reshape(shape[0] // 2, 2, shape[1] // 2, 2, shape[2]).mean(axis=(1, 3))

def prolong(field):
    return jnp.repeat(jnp.repeat(field, 2, axis=0), 2, axis=1)

def cycle(source, stencils, face_mask, height):
    tally = face_tally(source.shape, face_mask)
    if height == LEVELS:
        weights = stencils[2 * LEVELS]
        iterate = smooth(source, weights)
        for sweep_index in range(SWEEPS - 1):
            iterate = iterate + smooth(source - operate(iterate, tally), weights)
        return iterate
    presmooth = smooth(source, stencils[height])
    coarse = cycle(restrict(source - operate(presmooth, tally)), stencils, face_mask, height + 1)
    middle = presmooth + prolong(coarse)
    return middle + smooth(source - operate(middle, tally), stencils[LEVELS + height])

def reference(rhs, target, stencils, face_mask):
    solution, pullback = jax.vjp(lambda source, weights: cycle(source, weights, face_mask, 0), rhs, stencils)
    error = solution - target
    grad_rhs, grad_weights = pullback(error)
    return (solution, grad_rhs, grad_weights / CELLS)
```

```python
import functools

import jax
import jax.numpy as jnp
from jax import lax
from jax.experimental import pallas as pl
from jax.experimental.pallas import tpu as pltpu
from jax.sharding import PartitionSpec as P

MESH = pl.DeviceIdType.MESH
LEVELS = 4
NZ = 128
CHUNK = 64
RIM = (3, 4, 5, 5, 7)
KNOWN = ((0, 0), (0, 0), (1, 0), (1, 1), (1, 1))
SCALES = tuple(4.0**level for level in range(LEVELS + 1))


def pieces(level, block, axis):
    rim = RIM[level]
    if level <= 1:
        return [(-1, block - rim, rim, False), (0, 0, block, False), (1, 0, rim, False)]
    if level == 2:
        if axis == 0:
            return [(-1, -1, 4, False), (0, -1, 6, False), (1, 1, 4, False)]
        return [(-1, 3, 5, False), (0, 0, 8, False), (1, 0, 5, False)]
    if level == 3:
        if axis == 0:
            return [(-2, -1, 4, True), (0, -1, 4, False), (2, -1, 4, True)]
        return [(-1, -1, 4, False), (0, -1, 6, False), (1, 1, 4, False)]
    if axis == 0:
        return [(d, -1, 3, d != 0) for d in (-6, -3, 0, 3, 6)]
    return [(-3, -1, 2, False), (-2, -1, 4, True), (0, -1, 4, False), (2, -1, 4, True), (3, 1, 2, False)]


class Level:
    def __init__(self, level, block):
        self.index = level
        self.rows, self.cols = block
        self.rim = RIM[level]
        self.high = self.rows + 2 * self.rim
        self.pitch = self.cols + 2 * self.rim
        self.store = self.high + 1
        while self.store * self.pitch % 8:
            self.store += 1
        known_rows, known_cols = KNOWN[level]
        self.pad_rows = known_rows + (self.rows if level >= 3 else 0)
        self.pad_cols = known_cols + (self.cols if level >= 4 else 0)
        self.stage_rows = self.rows + 2 * self.pad_rows
        self.stage_pitch = -(-(self.cols + 2 * self.pad_cols) // 8) * 8
        self.cuts = (pieces(level, self.rows, 0), pieces(level, self.cols, 1))
        received = sum(n for d, s, n, w in self.cuts[0]) * sum(n for d, s, n, w in self.cuts[1])
        own = [n for d, s, n, w in self.cuts[0] if d == 0][0] * [n for d, s, n, w in self.cuts[1] if d == 0][0]
        assert received == self.high * self.pitch
        self.arriving = received - own

    def span(self, depth):
        return depth * self.pitch + depth, (self.high - depth - 1) * self.pitch + self.pitch - depth


def blocks(first, last, body, chunk=CHUNK):
    count = last - first
    chunk = min(chunk, count)
    steps = -(-count // chunk)
    if steps <= 2:
        for step in range(steps):
            body(min(first + step * chunk, last - chunk), chunk)
        return

    def one(step, carry):
        body(jnp.minimum(first + step * chunk, last - chunk), chunk)
        return carry

    lax.fori_loop(0, steps, one, 0)


def lanes(shape):
    return lax.broadcasted_iota(jnp.int32, shape, 1)


def from_below(v):
    return jnp.where(lanes(v.shape) == 0, 0.0, pltpu.roll(v, 1, 1))


def from_above(v):
    return jnp.where(lanes(v.shape) == NZ - 1, 0.0, pltpu.roll(v, NZ - 1, 1))


def stencil_at(src, weight, pitch, row, rows):
    sums = [None, None, None]
    for a in range(3):
        for b in range(3):
            v = src[pl.ds(row + (a - 1) * pitch + b - 1, rows), :]
            for c in range(3):
                term = weight(9 * a + 3 * b + c) * v
                sums[c] = term if sums[c] is None else sums[c] + term
    return sums[1] + from_below(sums[0]) + from_above(sums[2])


def operate_at(src, diag, pitch, row, rows):
    v = src[pl.ds(row, rows), :]
    beside = (src[pl.ds(row - pitch, rows), :] + src[pl.ds(row + pitch, rows), :]) + (
        src[pl.ds(row - 1, rows), :] + src[pl.ds(row + 1, rows), :]
    )
    return diag[pl.ds(row, rows), :] * v - (beside + (from_below(v) + from_above(v)))


def smooth(dst, src, weight, lv, depth, mask=None, add=None):
    def body(row, rows):
        value = stencil_at(src, weight, lv.pitch, row, rows)
        if add is not None:
            value = value + add[pl.ds(row, rows), :]
        if mask is not None:
            value = value * mask[pl.ds(row, rows), :]
        dst[pl.ds(row, rows), :] = value

    blocks(*lv.span(depth), body)


def remain(dst, src, field, diag, mask, lv, depth):
    def body(row, rows):
        value = src[pl.ds(row, rows), :] - operate_at(field, diag, lv.pitch, row, rows)
        dst[pl.ds(row, rows), :] = value * mask[pl.ds(row, rows), :]

    blocks(*lv.span(depth), body)


def restrict(stage, fine, lv, below):
    known_rows, known_cols = KNOWN[below.index]
    first = -known_cols
    starts = range(first, below.cols + known_cols, 8)

    def body(step, carry):
        for start in starts:
            row = (lv.rim + 2 * (step - known_rows)) * lv.pitch + lv.rim + 2 * start
            total = (fine[pl.ds(row, 8, stride=2), :] + fine[pl.ds(row + 1, 8, stride=2), :]) + (
                fine[pl.ds(row + lv.pitch, 8, stride=2), :] + fine[pl.ds(row + lv.pitch + 1, 8, stride=2), :]
            )
            at = (below.pad_rows - known_rows + step) * below.stage_pitch + below.pad_cols + start
            width = min(8, below.cols + known_cols - start)
            stage[pl.ds(at, width), :] = 0.25 * total[:width]
        return carry

    count = below.rows + 2 * known_rows
    if count <= 4:
        for step in range(count):
            body(step, 0)
    else:
        lax.fori_loop(0, count, body, 0)


def prolong_onto(dst, base, coarse, lv, below):
    half = 1 if lv.index == 0 else 2
    first, last = -half, below.cols + half
    starts = []
    start = first
    while True:
        if last - start <= 8:
            starts.append(max(first, last - 8))
            break
        starts.append(start)
        start += 8

    def body(step, carry):
        line = step - half
        values = [
            coarse[pl.ds((below.rim + line) * below.pitch + below.rim + start, 8), :] for start in starts
        ]
        for part in range(2):
            for start, value in zip(starts, values):
                row = (lv.rim + 2 * line + part) * lv.pitch + lv.rim + 2 * start
                for side in range(2):
                    where = pl.ds(row + side, 8, stride=2)
                    dst[where, :] = base[where, :] + value
        return carry

    count = below.rows + 2 * half
    lax.fori_loop(0, count, body, 0)


def folded(v):
    rows = v.shape[0]
    total = v[0:8]
    for at in range(8, rows, 8):
        total = total + v[at : at + 8]
    return total


def products(cot, cot_first, cot_pitch, field, lv, totals=None):
    width = max(8, lv.cols)
    keep = None
    if lv.cols < 8:
        keep = lax.broadcasted_iota(jnp.int32, (8, NZ), 0) < lv.cols

    def body(step, totals):
        here = cot[pl.ds(cot_first + step * cot_pitch, width), :]
        if keep is not None:
            here = jnp.where(keep, here, 0.0)
        turned = (from_above(here), here, from_below(here))
        out = []
        for a in range(3):
            for b in range(3):
                v = field[pl.ds((lv.rim + step + a - 1) * lv.pitch + lv.rim + b - 1, width), :]
                for c in range(3):
                    out.append(totals[len(out)] + folded(turned[c] * v))
        return tuple(out)

    if totals is None:
        totals = tuple(jnp.zeros((8, NZ), jnp.float32) for _ in range(27))
    if lv.rows <= 2:
        for step in range(lv.rows):
            totals = body(step, totals)
        return totals
    return lax.fori_loop(0, lv.rows, body, totals)


def keep_sums(sums, totals, row):
    for entry, total in enumerate(totals):
        sums[pl.ds(row * 32 + entry, 1), :] = jnp.sum(total, axis=0, keepdims=True)


def kernel(gx_size, gy_size, lvs, rhs, target, stencils, walls, solution_out, grad_out, weights_out, *scratch):
    scratch = list(scratch)
    take = lambda: scratch.pop(0)
    src = [[take() for _ in lvs] for _ in range(2)]
    aft = [[take() for _ in lvs] for _ in range(2)]
    pre = [take() for _ in lvs]
    mid = [take() for _ in lvs]
    out = [take() for _ in lvs]
    mask = [take() for _ in lvs]
    diag = [take() for _ in lvs]
    stage = [take() for _ in lvs]
    last_rest = [take() for _ in range(2)]
    goal, result, grad, sums, mine, over_y, over_x = (take() for _ in range(7))
    recv, send, local, io, reduce_send, reduce_recv = (take() for _ in range(6))

    gx, gy = lax.axis_index("gx"), lax.axis_index("gy")

    def flat(ref, lv):
        return ref.reshape(2 * lv.stage_rows * lv.stage_pitch, NZ)

    stages = [flat(stage[i], lv) for i, lv in enumerate(lvs)]
    blocks3 = [[src[way][i].reshape(lv.store, lv.pitch, NZ) for i, lv in enumerate(lvs)] for way in range(2)]

    def device(x, y):
        return (lax.rem(x + 2 * gx_size, gx_size), lax.rem(y + 2 * gy_size, gy_size))

    load_target = pltpu.make_async_copy(target, goal, io.at[0])
    load_target.start()
    for i, lv in enumerate(lvs):
        rows = lv.stage_rows * lv.stage_pitch
        first = rows if i < 2 else 0

        def clear(row, count, i=i):
            stages[i][pl.ds(row, count), :] = jnp.zeros((count, NZ), jnp.float32)

        blocks(first, 2 * rows, clear)
    load_rhs = pltpu.make_async_copy(rhs, stage[0].at[0], io.at[1])
    load_rhs.start()

    barrier = pltpu.get_barrier_semaphore()
    near = [(d, e) for d in (-2, -1, 0, 1, 2) for e in (-1, 0, 1) if (d, e) != (0, 0)]
    near = sorted(set((d % gx_size, e % gy_size) for d, e in near))
    for d, e in near:
        pl.semaphore_signal(barrier, inc=1, device_id=device(gx + d, gy + e), device_id_type=MESH)

    def lay_out(i):
        lv = lvs[i]
        wall = [walls[k].astype(jnp.float32) for k in range(6)]
        total_rows, total_cols = gx_size * lv.rows, gy_size * lv.cols
        starts = list(range(0, lv.pitch, 8))

        def body(step, carry):
            line = gx * lv.rows - lv.rim + step
            first = jnp.where(line == 0, wall[0], 0.0) + jnp.where(line == total_rows - 1, wall[1], 0.0)
            within = (line >= 0) & (line < total_rows)
            for start in starts:
                column = gy * lv.cols - lv.rim + start + lax.broadcasted_iota(jnp.int32, (8, NZ), 0)
                lane = lanes((8, NZ))
                tally = first + jnp.where(column == 0, wall[2], 0.0) + jnp.where(column == total_cols - 1, wall[3], 0.0)
                tally = tally + jnp.where(lane == 0, wall[4], 0.0) + jnp.where(lane == NZ - 1, wall[5], 0.0)
                inside = (column >= 0) & (column < total_cols) & within
                where = pl.ds(step * lv.pitch + start, 8)
                diag[i][where, :] = 6.0 - tally
                mask[i][where, :] = jnp.where(inside, 1.0, 0.0)
            return carry

        lax.fori_loop(0, lv.high, body, 0)

    def placed(cut, me, size, block, known):
        offset, first, count, inward = cut
        if inward:
            low = offset > 0
            swapped = (me == 0) if low else (me == size - 1)
            step = -1 if low else 1
            acting = jnp.where(swapped, me + step, me)
            mirrored = jnp.where(swapped, -offset, offset)
            other = block - first - count
            begin = jnp.where(swapped, other + step * block, first)
            start = jnp.where(swapped, other, first)
        else:
            acting, mirrored, begin, start = me, offset, first, first
        to = acting - mirrored
        outside = (to < 0) | (to >= size)
        return begin, to, mirrored * block + start, outside, count

    def exchange(way, i):
        lv = lvs[i]
        for cut_x in lv.cuts[0]:
            begin_x, to_x, land_x, out_x, count_x = placed(cut_x, gx, gx_size, lv.rows, 0)
            for cut_y in lv.cuts[1]:
                begin_y, to_y, land_y, out_y, count_y = placed(cut_y, gy, gy_size, lv.cols, 0)
                dst = blocks3[way][i].at[pl.ds(lv.rim + land_x, count_x), pl.ds(lv.rim + land_y, count_y)]
                if cut_x[0] == 0 and cut_y[0] == 0:
                    piece = stage[i].at[
                        0, pl.ds(lv.pad_rows + begin_x, count_x), pl.ds(lv.pad_cols + begin_y, count_y)
                    ]
                    pltpu.make_async_copy(piece, dst, local.at[way, i]).start()
                    continue
                piece = stage[i].at[
                    jnp.where(out_x | out_y, 1, 0),
                    pl.ds(lv.pad_rows + begin_x, count_x),
                    pl.ds(lv.pad_cols + begin_y, count_y),
                ]
                pltpu.make_async_remote_copy(
                    src_ref=piece,
                    dst_ref=dst,
                    send_sem=send.at[way, i],
                    recv_sem=recv.at[way, i],
                    device_id=device(to_x, to_y),
                    device_id_type=MESH,
                ).start()

    def await_bytes(ref, rows, sem):
        pltpu.make_async_copy(ref.at[pl.ds(0, rows)], ref.at[pl.ds(0, rows)], sem).wait()

    def arrived(way, i):
        lv = lvs[i]
        await_bytes(src[way][i], lv.arriving, recv.at[way, i])
        await_bytes(src[way][i], lv.high * lv.pitch - lv.arriving, local.at[way, i])

    def sent(way, i):
        await_bytes(src[way][i], lvs[i].arriving, send.at[way, i])

    def weights(way, row):
        if way == 0:
            return lambda entry: stencils[row, entry]
        return lambda entry: stencils[row, 26 - entry]

    def cycle(way, waiting):
        for i in range(LEVELS):
            lv = lvs[i]
            exchange(way, i)
            waiting(i)
            arrived(way, i)
            smooth(pre[i], src[way][i], weights(way, i if way == 0 else LEVELS + i), lv, 1, mask[i])
            known = max(KNOWN[i + 1])
            remain(mid[i], src[way][i], pre[i], diag[i], mask[i], lv, lv.rim - 2 * known)
            sent(way, i)
            if way == 1 and i + 1 == LEVELS:
                sent(0, LEVELS)
            restrict(stages[i + 1], mid[i], lv, lvs[i + 1])
        bottom = lvs[LEVELS]
        weight = weights(way, 2 * LEVELS)
        exchange(way, LEVELS)
        waiting(LEVELS)
        arrived(way, LEVELS)
        b = src[way][LEVELS]
        x, y = pre[LEVELS], mid[LEVELS]
        rest = (aft[way][LEVELS], last_rest[way])
        smooth(x, b, weight, bottom, 1, mask[LEVELS])
        remain(rest[0], b, x, diag[LEVELS], mask[LEVELS], bottom, 2)
        smooth(y, rest[0], weight, bottom, 3, mask[LEVELS], x)
        remain(rest[1], b, y, diag[LEVELS], mask[LEVELS], bottom, 4)
        smooth(out[LEVELS], rest[1], weight, bottom, 5, mask[LEVELS], y)
        if way == 1:
            sent(1, LEVELS)
        for i in reversed(range(LEVELS)):
            lv = lvs[i]
            prolong_onto(mid[i], pre[i], out[i + 1], lv, lvs[i + 1])
            remain(aft[way][i], src[way][i], mid[i], diag[i], mask[i], lv, 2)
            if i > 0:
                smooth(out[i], aft[way][i], weights(way, LEVELS + i if way == 0 else i), lv, 3, mask[i], mid[i])

    def finish(weight, way, store):
        lv = lvs[0]

        def body(step, carry):
            row = (lv.rim + step) * lv.pitch + lv.rim
            value = stencil_at(aft[way][0], weight, lv.pitch, row, lv.cols)
            store(step, value + mid[0][pl.ds(row, lv.cols), :])
            return carry

        lax.fori_loop(0, lv.rows, body, 0)

    lay_out(0)
    load_rhs.wait()
    pl.semaphore_wait(barrier, len(near))

    def forward_waits(i):
        if i == 0:
            for level in range(1, LEVELS + 1):
                lay_out(level)
            rows = sums.shape[0]
            sums[...] = jnp.zeros((rows, NZ), jnp.float32)

    cycle(0, forward_waits)

    load_target.wait()

    def store_solution(step, value):
        result[step] = value
        stage[0][0, step] = value - goal[step]

    finish(weights(0, LEVELS), 0, store_solution)
    save_solution = pltpu.make_async_copy(result, solution_out, io.at[2])
    save_solution.start()

    def backward_waits(i):
        lv = lvs[i]
        if i < LEVELS:
            first = lv.pad_rows * lv.stage_pitch + lv.pad_cols
            keep_sums(sums, products(stages[i], first, lv.stage_pitch, aft[0][i], lv), LEVELS + i)

    cycle(1, backward_waits)

    bottom = lvs[LEVELS]
    at = bottom.rim * bottom.pitch + bottom.rim
    totals = products(src[1][LEVELS], at, bottom.pitch, last_rest[0], bottom)
    totals = products(aft[1][LEVELS], at, bottom.pitch, aft[0][LEVELS], bottom, totals)
    totals = products(last_rest[1], at, bottom.pitch, src[0][LEVELS], bottom, totals)
    keep_sums(sums, totals, 2 * LEVELS)
    for i in reversed(range(LEVELS)):
        lv = lvs[i]
        at = lv.rim * lv.pitch + lv.rim
        keep_sums(sums, products(aft[1][i], at, lv.pitch, src[0][i], lv), i)

    ones = jnp.ones((8, NZ), jnp.float32)
    for part in range(3):
        line = lax.dot_general(
            ones,
            sums[pl.ds(part * NZ, NZ), :],
            (((1,), (1,)), ((), ())),
            precision=lax.Precision.HIGHEST,
            preferred_element_type=jnp.float32,
        )
        mine[0, pl.ds(part, 1), :] = line[0:1]

    def spread(slot, held, me, size, where):
        source = mine.at[slot, pl.ds(0, 3)]
        for step in range(1, size):
            pltpu.make_async_remote_copy(
                src_ref=source,
                dst_ref=held.at[me, pl.ds(0, 3)],
                send_sem=reduce_send.at[slot],
                recv_sem=reduce_recv.at[slot],
                device_id=where(step),
                device_id_type=MESH,
            ).start()
        held[me] = mine[slot]

    def gathered(slot, held, size):
        await_bytes(src[0][0], 3 * (size - 1), reduce_recv.at[slot])
        total = held[0]
        for step in range(1, size):
            total = total + held[step]
        return total

    spread(0, over_y, gy, gy_size, lambda step: device(gx, gy + step))

    def store_grad(step, value):
        grad[step] = value

    finish(weights(1, 0), 1, store_grad)
    save_grad = pltpu.make_async_copy(grad, grad_out, io.at[3])
    save_grad.start()

    mine[1] = gathered(0, over_y, gy_size)
    spread(1, over_x, gx, gx_size, lambda step: device(gx + step, gy))
    await_bytes(src[0][0], 3 * (gy_size - 1), reduce_send.at[0])
    save_solution.wait()
    save_grad.wait()
    total = gathered(1, over_x, gx_size)
    await_bytes(src[0][0], 3 * (gx_size - 1), reduce_send.at[1])
    cells = gx_size * lvs[0].rows * gy_size * lvs[0].cols * NZ
    for row in range(2 * LEVELS + 1):
        scale = SCALES[row % LEVELS if row < 2 * LEVELS else LEVELS] / cells
        part, lane = row // 4, 32 * (row % 4)
        weights_out[pl.ds(row, 1), :] = total[part : part + 1, lane : lane + 27] * scale


def on_device(gx_size, gy_size, rhs, target, stencils, face_mask):
    rows, cols, _ = rhs.shape
    lvs = [Level(i, (rows >> i, cols >> i)) for i in range(LEVELS + 1)]
    field = lambda lv: pltpu.VMEM((lv.store * lv.pitch, NZ), jnp.float32)
    scratch = []
    for _ in range(9):
        scratch += [field(lv) for lv in lvs]
    scratch += [pltpu.VMEM((2, lv.stage_rows, lv.stage_pitch, NZ), jnp.float32) for lv in lvs]
    scratch += [field(lvs[LEVELS])] * 2
    scratch += [pltpu.VMEM((rows, cols, NZ), jnp.float32)] * 3
    scratch += [
        pltpu.VMEM((3 * NZ, NZ), jnp.float32),
        pltpu.VMEM((2, 8, NZ), jnp.float32),
        pltpu.VMEM((gy_size, 8, NZ), jnp.float32),
        pltpu.VMEM((gx_size, 8, NZ), jnp.float32),
        pltpu.SemaphoreType.DMA((2, LEVELS + 1)),
        pltpu.SemaphoreType.DMA((2, LEVELS + 1)),
        pltpu.SemaphoreType.DMA((2, LEVELS + 1)),
        pltpu.SemaphoreType.DMA((4,)),
        pltpu.SemaphoreType.DMA((2,)),
        pltpu.SemaphoreType.DMA((2,)),
    ]
    return pl.pallas_call(
        functools.partial(kernel, gx_size, gy_size, lvs),
        out_shape=(
            jax.ShapeDtypeStruct(rhs.shape, jnp.float32),
            jax.ShapeDtypeStruct(rhs.shape, jnp.float32),
            jax.ShapeDtypeStruct(stencils.shape, jnp.float32),
        ),
        in_specs=[
            pl.BlockSpec(memory_space=pl.ANY),
            pl.BlockSpec(memory_space=pl.ANY),
            pl.BlockSpec(memory_space=pltpu.SMEM),
            pl.BlockSpec(memory_space=pltpu.SMEM),
        ],
        out_specs=(
            pl.BlockSpec(memory_space=pl.ANY),
            pl.BlockSpec(memory_space=pl.ANY),
            pl.BlockSpec(memory_space=pltpu.VMEM),
        ),
        scratch_shapes=scratch,
        compiler_params=pltpu.CompilerParams(
            collective_id=0, has_side_effects=True, vmem_limit_bytes=40 << 20
        ),
        cost_estimate=pl.CostEstimate(flops=60_000_000, bytes_accessed=1_100_000, transcendentals=0),
    )(rhs, target, stencils, face_mask)


def solution(mesh):
    sizes = dict(mesh.shape)
    return jax.shard_map(
        functools.partial(on_device, sizes["gx"], sizes["gy"]),
        mesh=mesh,
        in_specs=(P("gx", "gy", None), P("gx", "gy", None), P(), P()),
        out_specs=(P("gx", "gy", None), P("gx", "gy", None), P()),
        check_vma=False,
    )
```

```python
import functools

import jax
import jax.numpy as jnp
from jax import lax
from jax.experimental import pallas as pl
from jax.experimental.pallas import tpu as pltpu
from jax.sharding import PartitionSpec as P

MESH = pl.DeviceIdType.MESH
LEVELS = 4
NZ = 128
CHUNK = 384
UNROLL = 8
RIM = (3, 4, 5, 5, 7)
KNOWN = ((0, 0), (0, 0), (1, 0), (1, 1), (1, 1))
SCALES = tuple(4.0**level for level in range(LEVELS + 1))


def pieces(level, block, axis):
    rim = RIM[level]
    if level <= 1:
        return [(-1, block - rim, rim, False), (0, 0, block, False), (1, 0, rim, False)]
    if level == 2:
        if axis == 0:
            return [(-1, -1, 4, False), (0, -1, 6, False), (1, 1, 4, False)]
        return [(-1, 3, 5, False), (0, 0, 8, False), (1, 0, 5, False)]
    if level == 3:
        if axis == 0:
            return [(-2, -1, 4, True), (0, -1, 4, False), (2, -1, 4, True)]
        return [(-1, -1, 4, False), (0, -1, 6, False), (1, 1, 4, False)]
    if axis == 0:
        return [(d, -1, 3, d != 0) for d in (-6, -3, 0, 3, 6)]
    return [(-3, -1, 2, False), (-2, -1, 4, True), (0, -1, 4, False), (2, -1, 4, True), (3, 1, 2, False)]


class Level:
    def __init__(self, level, block):
        self.index = level
        self.rows, self.cols = block
        self.rim = RIM[level]
        self.high = self.rows + 2 * self.rim
        self.pitch = self.cols + 2 * self.rim
        self.store = self.high + 1
        while self.store * self.pitch % 8:
            self.store += 1
        known_rows, known_cols = KNOWN[level]
        self.pad_rows = known_rows + (self.rows if level >= 3 else 0)
        self.pad_cols = known_cols + (self.cols if level >= 4 else 0)
        self.stage_rows = self.rows + 2 * self.pad_rows
        self.stage_pitch = -(-(self.cols + 2 * self.pad_cols) // 8) * 8
        self.cuts = (pieces(level, self.rows, 0), pieces(level, self.cols, 1))
        received = sum(n for d, s, n, w in self.cuts[0]) * sum(n for d, s, n, w in self.cuts[1])
        own = [n for d, s, n, w in self.cuts[0] if d == 0][0] * [n for d, s, n, w in self.cuts[1] if d == 0][0]
        assert received == self.high * self.pitch
        self.arriving = received - own

    def span(self, depth):
        return depth * self.pitch + depth, (self.high - depth - 1) * self.pitch + self.pitch - depth


def blocks(first, last, body, chunk=CHUNK):
    count = last - first
    chunk = min(chunk, count)
    steps = -(-count // chunk)
    if steps <= 2:
        for step in range(steps):
            body(min(first + step * chunk, last - chunk), chunk)
        return

    def one(step, carry):
        body(jnp.minimum(first + step * chunk, last - chunk), chunk)
        return carry

    lax.fori_loop(0, steps, one, 0)


def hops_x(offset):
    return min(abs(offset), 8 - abs(offset)) + (offset != 0)


def hops_y(offset):
    return abs(offset) / 2


def lanes(shape):
    return lax.broadcasted_iota(jnp.int32, shape, 1)


def from_below(v):
    return jnp.where(lanes(v.shape) == 0, 0.0, pltpu.roll(v, 1, 1))


def from_above(v):
    return jnp.where(lanes(v.shape) == NZ - 1, 0.0, pltpu.roll(v, NZ - 1, 1))


def stencil_at(src, weight, pitch, row, rows):
    sums = [None, None, None]
    for a in range(3):
        for b in range(3):
            v = src[pl.ds(row + (a - 1) * pitch + b - 1, rows), :]
            for c in range(3):
                term = weight(9 * a + 3 * b + c) * v
                sums[c] = term if sums[c] is None else sums[c] + term
    return sums[1] + from_below(sums[0]) + from_above(sums[2])


def operate_at(src, diag, pitch, row, rows):
    v = src[pl.ds(row, rows), :]
    beside = (src[pl.ds(row - pitch, rows), :] + src[pl.ds(row + pitch, rows), :]) + (
        src[pl.ds(row - 1, rows), :] + src[pl.ds(row + 1, rows), :]
    )
    return diag[pl.ds(row, rows), :] * v - (beside + (from_below(v) + from_above(v)))


def smooth(dst, src, weight, lv, depth, mask=None, add=None):
    def body(row, rows):
        value = stencil_at(src, weight, lv.pitch, row, rows)
        if add is not None:
            value = value + add[pl.ds(row, rows), :]
        if mask is not None:
            value = value * mask[pl.ds(row, rows), :]
        dst[pl.ds(row, rows), :] = value

    blocks(*lv.span(depth), body)


def remain(dst, src, field, diag, mask, lv, depth):
    def body(row, rows):
        value = src[pl.ds(row, rows), :] - operate_at(field, diag, lv.pitch, row, rows)
        dst[pl.ds(row, rows), :] = value * mask[pl.ds(row, rows), :]

    blocks(*lv.span(depth), body)


def restrict(stage, fine, lv, below):
    known_rows, known_cols = KNOWN[below.index]
    first = -known_cols
    starts = range(first, below.cols + known_cols, 8)

    def body(step, carry):
        for start in starts:
            row = (lv.rim + 2 * (step - known_rows)) * lv.pitch + lv.rim + 2 * start
            total = (fine[pl.ds(row, 8, stride=2), :] + fine[pl.ds(row + 1, 8, stride=2), :]) + (
                fine[pl.ds(row + lv.pitch, 8, stride=2), :] + fine[pl.ds(row + lv.pitch + 1, 8, stride=2), :]
            )
            at = (below.pad_rows - known_rows + step) * below.stage_pitch + below.pad_cols + start
            width = min(8, below.cols + known_cols - start)
            stage[pl.ds(at, width), :] = 0.25 * total[:width]
        return carry

    count = below.rows + 2 * known_rows
    if count <= 4:
        for step in range(count):
            body(step, 0)
    else:
        lax.fori_loop(0, count, body, 0)


def prolong_onto(dst, base, coarse, lv, below):
    half = 1 if lv.index == 0 else 2
    first, last = -half, below.cols + half
    starts = []
    start = first
    while True:
        if last - start <= 8:
            starts.append(max(first, last - 8))
            break
        starts.append(start)
        start += 8

    def body(step, carry):
        line = step - half
        values = [
            coarse[pl.ds((below.rim + line) * below.pitch + below.rim + start, 8), :] for start in starts
        ]
        for part in range(2):
            for start, value in zip(starts, values):
                row = (lv.rim + 2 * line + part) * lv.pitch + lv.rim + 2 * start
                for side in range(2):
                    where = pl.ds(row + side, 8, stride=2)
                    dst[where, :] = base[where, :] + value
        return carry

    count = below.rows + 2 * half
    lax.fori_loop(0, count, body, 0)


def folded(v):
    rows = v.shape[0]
    total = v[0:8]
    for at in range(8, rows, 8):
        total = total + v[at : at + 8]
    return total


def products(cot, cot_first, cot_pitch, field, lv, totals=None):
    width = max(8, lv.cols)
    keep = None
    if lv.cols < 8:
        keep = lax.broadcasted_iota(jnp.int32, (8, NZ), 0) < lv.cols

    def body(step, totals):
        here = cot[pl.ds(cot_first + step * cot_pitch, width), :]
        if keep is not None:
            here = jnp.where(keep, here, 0.0)
        turned = (from_above(here), here, from_below(here))
        out = []
        for a in range(3):
            for b in range(3):
                v = field[pl.ds((lv.rim + step + a - 1) * lv.pitch + lv.rim + b - 1, width), :]
                for c in range(3):
                    out.append(totals[len(out)] + folded(turned[c] * v))
        return tuple(out)

    if totals is None:
        totals = tuple(jnp.zeros((8, NZ), jnp.float32) for _ in range(27))
    if lv.rows <= 2:
        for step in range(lv.rows):
            totals = body(step, totals)
        return totals
    unroll = min(UNROLL, lv.rows)

    def several(step, totals):
        for part in range(unroll):
            totals = body(step * unroll + part, totals)
        return totals

    return lax.fori_loop(0, lv.rows // unroll, several, totals)


def keep_sums(sums, totals, row):
    for entry, total in enumerate(totals):
        sums[pl.ds(row * 32 + entry, 1), :] = jnp.sum(total, axis=0, keepdims=True)


def kernel(gx_size, gy_size, lvs, rhs, target, stencils_in, walls_in, solution_out, grad_out, weights_out, *scratch):
    scratch = list(scratch)
    take = lambda: scratch.pop(0)
    src = [[take() for _ in lvs] for _ in range(2)]
    aft = [[take() for _ in lvs] for _ in range(2)]
    pre = [take() for _ in lvs]
    mid = [take() for _ in lvs]
    out = [take() for _ in lvs]
    mask = [take() for _ in lvs]
    diag = [take() for _ in lvs]
    stage = [take() for _ in lvs]
    last_rest = [take() for _ in range(2)]
    goal, result, grad, sums, mine, over_y, over_x = (take() for _ in range(7))
    stencils, walls = take(), take()
    recv, send, local, io, reduce_send, reduce_recv = (take() for _ in range(6))

    gx, gy = lax.axis_index("gx"), lax.axis_index("gy")

    def flat(ref, lv):
        return ref.reshape(2 * lv.stage_rows * lv.stage_pitch, NZ)

    stages = [flat(stage[i], lv) for i, lv in enumerate(lvs)]
    blocks3 = [[src[way][i].reshape(lv.store, lv.pitch, NZ) for i, lv in enumerate(lvs)] for way in range(2)]

    def device(x, y):
        return (lax.rem(x + 2 * gx_size, gx_size), lax.rem(y + 2 * gy_size, gy_size))

    load_target = pltpu.make_async_copy(target, goal, io.at[0])
    load_target.start()
    load_walls = pltpu.make_async_copy(walls_in, walls, io.at[4])
    load_walls.start()
    load_stencils = pltpu.make_async_copy(stencils_in, stencils, io.at[5])
    load_stencils.start()
    for i, lv in enumerate(lvs):
        rows = lv.stage_rows * lv.stage_pitch
        first = rows if i < 2 else 0

        def clear(row, count, i=i):
            stages[i][pl.ds(row, count), :] = jnp.zeros((count, NZ), jnp.float32)

        blocks(first, 2 * rows, clear)
    load_rhs = pltpu.make_async_copy(rhs, stage[0].at[0], io.at[1])
    load_rhs.start()

    barrier = pltpu.get_barrier_semaphore()
    near = [(d, e) for d in (-2, -1, 0, 1, 2) for e in (-1, 0, 1) if (d, e) != (0, 0)]
    near = sorted(set((d % gx_size, e % gy_size) for d, e in near))
    for d, e in near:
        pl.semaphore_signal(barrier, inc=1, device_id=device(gx + d, gy + e), device_id_type=MESH)

    def lay_out(i):
        lv = lvs[i]
        wall = [walls[k].astype(jnp.float32) for k in range(6)]
        total_rows, total_cols = gx_size * lv.rows, gy_size * lv.cols
        starts = list(range(0, lv.pitch, 8))

        def body(step, carry):
            line = gx * lv.rows - lv.rim + step
            first = jnp.where(line == 0, wall[0], 0.0) + jnp.where(line == total_rows - 1, wall[1], 0.0)
            within = (line >= 0) & (line < total_rows)
            for start in starts:
                column = gy * lv.cols - lv.rim + start + lax.broadcasted_iota(jnp.int32, (8, NZ), 0)
                lane = lanes((8, NZ))
                tally = first + jnp.where(column == 0, wall[2], 0.0) + jnp.where(column == total_cols - 1, wall[3], 0.0)
                tally = tally + jnp.where(lane == 0, wall[4], 0.0) + jnp.where(lane == NZ - 1, wall[5], 0.0)
                inside = (column >= 0) & (column < total_cols) & within
                where = pl.ds(step * lv.pitch + start, 8)
                diag[i][where, :] = 6.0 - tally
                mask[i][where, :] = jnp.where(inside, 1.0, 0.0)
            return carry

        lax.fori_loop(0, lv.high, body, 0)

    def placed(cut, me, size, block):
        offset, first, count, inward = cut
        if inward:
            low = offset > 0
            swapped = (me == 0) if low else (me == size - 1)
            step = -1 if low else 1
            acting = jnp.where(swapped, me + step, me)
            mirrored = jnp.where(swapped, -offset, offset)
            other = block - first - count
            begin = jnp.where(swapped, other + step * block, first)
            start = jnp.where(swapped, other, first)
        else:
            acting, mirrored, begin, start = me, offset, first, first
        to = acting - mirrored
        outside = (to < 0) | (to >= size)
        return begin, to, mirrored * block + start, outside, count

    def exchange(way, i):
        lv = lvs[i]
        across = [placed(cut, gx, gx_size, lv.rows) for cut in lv.cuts[0]]
        along = [placed(cut, gy, gy_size, lv.cols) for cut in lv.cuts[1]]
        pairs = [(p, q) for p in range(len(across)) for q in range(len(along))]
        pairs.sort(key=lambda pq: -(hops_x(lv.cuts[0][pq[0]][0]) + hops_y(lv.cuts[1][pq[1]][0])))
        for p, q in pairs:
            cut_x, cut_y = lv.cuts[0][p], lv.cuts[1][q]
            begin_x, to_x, land_x, out_x, count_x = across[p]
            begin_y, to_y, land_y, out_y, count_y = along[q]
            dst = blocks3[way][i].at[pl.ds(lv.rim + land_x, count_x), pl.ds(lv.rim + land_y, count_y)]
            if cut_x[0] == 0 and cut_y[0] == 0:
                piece = stage[i].at[
                    0, pl.ds(lv.pad_rows + begin_x, count_x), pl.ds(lv.pad_cols + begin_y, count_y)
                ]
                pltpu.make_async_copy(piece, dst, local.at[way, i]).start()
                continue
            piece = stage[i].at[
                jnp.where(out_x | out_y, 1, 0),
                pl.ds(lv.pad_rows + begin_x, count_x),
                pl.ds(lv.pad_cols + begin_y, count_y),
            ]
            pltpu.make_async_remote_copy(
                src_ref=piece,
                dst_ref=dst,
                send_sem=send.at[way, i],
                recv_sem=recv.at[way, i],
                device_id=device(to_x, to_y),
                device_id_type=MESH,
            ).start()

    def await_bytes(ref, rows, sem):
        pltpu.make_async_copy(ref.at[pl.ds(0, rows)], ref.at[pl.ds(0, rows)], sem).wait()

    def arrived(way, i):
        lv = lvs[i]
        await_bytes(src[way][i], lv.arriving, recv.at[way, i])
        await_bytes(src[way][i], lv.high * lv.pitch - lv.arriving, local.at[way, i])

    def sent(way, i):
        await_bytes(src[way][i], lvs[i].arriving, send.at[way, i])

    def weights(way, row):
        if way == 0:
            return lambda entry: stencils[row, entry]
        return lambda entry: stencils[row, 26 - entry]

    def cycle(way, waiting):
        for i in range(LEVELS):
            lv = lvs[i]
            exchange(way, i)
            waiting(i)
            arrived(way, i)
            smooth(pre[i], src[way][i], weights(way, i if way == 0 else LEVELS + i), lv, 1, mask[i])
            known = max(KNOWN[i + 1])
            remain(mid[i], src[way][i], pre[i], diag[i], mask[i], lv, lv.rim - 2 * known)
            sent(way, i)
            if way == 1 and i + 1 == LEVELS:
                sent(0, LEVELS)
            restrict(stages[i + 1], mid[i], lv, lvs[i + 1])
        bottom = lvs[LEVELS]
        weight = weights(way, 2 * LEVELS)
        exchange(way, LEVELS)
        waiting(LEVELS)
        arrived(way, LEVELS)
        b = src[way][LEVELS]
        x, y = pre[LEVELS], mid[LEVELS]
        rest = (aft[way][LEVELS], last_rest[way])
        smooth(x, b, weight, bottom, 1, mask[LEVELS])
        remain(rest[0], b, x, diag[LEVELS], mask[LEVELS], bottom, 2)
        smooth(y, rest[0], weight, bottom, 3, mask[LEVELS], x)
        remain(rest[1], b, y, diag[LEVELS], mask[LEVELS], bottom, 4)
        smooth(out[LEVELS], rest[1], weight, bottom, 5, mask[LEVELS], y)
        if way == 1:
            sent(1, LEVELS)
        for i in reversed(range(LEVELS)):
            lv = lvs[i]
            prolong_onto(mid[i], pre[i], out[i + 1], lv, lvs[i + 1])
            remain(aft[way][i], src[way][i], mid[i], diag[i], mask[i], lv, 2)
            if i > 0:
                smooth(out[i], aft[way][i], weights(way, LEVELS + i if way == 0 else i), lv, 3, mask[i], mid[i])

    def finish(weight, way, store):
        lv = lvs[0]

        def body(step, carry):
            for part in range(UNROLL):
                line = step * UNROLL + part
                row = (lv.rim + line) * lv.pitch + lv.rim
                value = stencil_at(aft[way][0], weight, lv.pitch, row, lv.cols)
                store(line, value + mid[0][pl.ds(row, lv.cols), :])
            return carry

        lax.fori_loop(0, lv.rows // UNROLL, body, 0)

    load_walls.wait()
    lay_out(0)
    load_stencils.wait()
    load_rhs.wait()
    pl.semaphore_wait(barrier, len(near))

    def forward_waits(i):
        if i == 0:
            for level in range(1, LEVELS + 1):
                lay_out(level)
            rows = sums.shape[0]
            sums[...] = jnp.zeros((rows, NZ), jnp.float32)

    cycle(0, forward_waits)

    load_target.wait()

    def store_solution(step, value):
        result[step] = value
        stage[0][0, step] = value - goal[step]

    finish(weights(0, LEVELS), 0, store_solution)
    save_solution = pltpu.make_async_copy(result, solution_out, io.at[2])
    save_solution.start()

    def backward_waits(i):
        lv = lvs[i]
        if i < LEVELS:
            first = lv.pad_rows * lv.stage_pitch + lv.pad_cols
            keep_sums(sums, products(stages[i], first, lv.stage_pitch, aft[0][i], lv), LEVELS + i)

    cycle(1, backward_waits)

    bottom = lvs[LEVELS]
    at = bottom.rim * bottom.pitch + bottom.rim
    totals = products(src[1][LEVELS], at, bottom.pitch, last_rest[0], bottom)
    totals = products(aft[1][LEVELS], at, bottom.pitch, aft[0][LEVELS], bottom, totals)
    totals = products(last_rest[1], at, bottom.pitch, src[0][LEVELS], bottom, totals)
    keep_sums(sums, totals, 2 * LEVELS)
    for i in reversed(range(LEVELS)):
        lv = lvs[i]
        at = lv.rim * lv.pitch + lv.rim
        keep_sums(sums, products(aft[1][i], at, lv.pitch, src[0][i], lv), i)

    ones = jnp.ones((8, NZ), jnp.float32)
    for part in range(3):
        line = lax.dot_general(
            ones,
            sums[pl.ds(part * NZ, NZ), :],
            (((1,), (1,)), ((), ())),
            precision=lax.Precision.HIGHEST,
            preferred_element_type=jnp.float32,
        )
        mine[0, pl.ds(part, 1), :] = line[0:1]

    def spread(slot, held, me, order, where):
        source = mine.at[slot, pl.ds(0, 3)]
        for step in order:
            pltpu.make_async_remote_copy(
                src_ref=source,
                dst_ref=held.at[me, pl.ds(0, 3)],
                send_sem=reduce_send.at[slot],
                recv_sem=reduce_recv.at[slot],
                device_id=where(step),
                device_id_type=MESH,
            ).start()
        held[me] = mine[slot]

    def gathered(slot, held, size):
        await_bytes(src[0][0], 3 * (size - 1), reduce_recv.at[slot])
        total = held[0]
        for step in range(1, size):
            total = total + held[step]
        return total

    order = sorted(range(1, gy_size), key=lambda step: -min(step, gy_size - step))
    spread(0, over_y, gy, order, lambda step: device(gx, gy + step))

    def store_grad(step, value):
        grad[step] = value

    finish(weights(1, 0), 1, store_grad)
    save_grad = pltpu.make_async_copy(grad, grad_out, io.at[3])
    save_grad.start()

    mine[1] = gathered(0, over_y, gy_size)
    order = sorted(range(1, gx_size), key=lambda step: -min(step % 8, 8 - step % 8) - min(step, gx_size - step) / 8)
    spread(1, over_x, gx, order, lambda step: device(gx + step, gy))
    await_bytes(src[0][0], 3 * (gy_size - 1), reduce_send.at[0])
    save_solution.wait()
    save_grad.wait()
    total = gathered(1, over_x, gx_size)
    await_bytes(src[0][0], 3 * (gx_size - 1), reduce_send.at[1])
    cells = gx_size * lvs[0].rows * gy_size * lvs[0].cols * NZ
    for row in range(2 * LEVELS + 1):
        scale = SCALES[row % LEVELS if row < 2 * LEVELS else LEVELS] / cells
        part, lane = row // 4, 32 * (row % 4)
        weights_out[pl.ds(row, 1), :] = total[part : part + 1, lane : lane + 27] * scale


def on_device(gx_size, gy_size, rhs, target, stencils, face_mask):
    rows, cols, _ = rhs.shape
    lvs = [Level(i, (rows >> i, cols >> i)) for i in range(LEVELS + 1)]
    field = lambda lv: pltpu.VMEM((lv.store * lv.pitch, NZ), jnp.float32)
    scratch = []
    for _ in range(9):
        scratch += [field(lv) for lv in lvs]
    scratch += [pltpu.VMEM((2, lv.stage_rows, lv.stage_pitch, NZ), jnp.float32) for lv in lvs]
    scratch += [field(lvs[LEVELS])] * 2
    scratch += [pltpu.VMEM((rows, cols, NZ), jnp.float32)] * 3
    scratch += [
        pltpu.VMEM((3 * NZ, NZ), jnp.float32),
        pltpu.VMEM((2, 8, NZ), jnp.float32),
        pltpu.VMEM((gy_size, 8, NZ), jnp.float32),
        pltpu.VMEM((gx_size, 8, NZ), jnp.float32),
        pltpu.SMEM(stencils.shape, jnp.float32),
        pltpu.SMEM(face_mask.shape, jnp.int32),
        pltpu.SemaphoreType.DMA((2, LEVELS + 1)),
        pltpu.SemaphoreType.DMA((2, LEVELS + 1)),
        pltpu.SemaphoreType.DMA((2, LEVELS + 1)),
        pltpu.SemaphoreType.DMA((6,)),
        pltpu.SemaphoreType.DMA((2,)),
        pltpu.SemaphoreType.DMA((2,)),
    ]
    return pl.pallas_call(
        functools.partial(kernel, gx_size, gy_size, lvs),
        out_shape=(
            jax.ShapeDtypeStruct(rhs.shape, jnp.float32),
            jax.ShapeDtypeStruct(rhs.shape, jnp.float32),
            jax.ShapeDtypeStruct(stencils.shape, jnp.float32),
        ),
        in_specs=[
            pl.BlockSpec(memory_space=pltpu.HBM),
            pl.BlockSpec(memory_space=pltpu.HBM),
            pl.BlockSpec(memory_space=pltpu.HBM),
            pl.BlockSpec(memory_space=pltpu.HBM),
        ],
        out_specs=(
            pl.BlockSpec(memory_space=pl.ANY),
            pl.BlockSpec(memory_space=pl.ANY),
            pl.BlockSpec(memory_space=pltpu.VMEM),
        ),
        scratch_shapes=scratch,
        compiler_params=pltpu.CompilerParams(
            collective_id=0, has_side_effects=True, vmem_limit_bytes=60 << 20
        ),
        cost_estimate=pl.CostEstimate(flops=60_000_000, bytes_accessed=1_100_000, transcendentals=0),
    )(rhs, target, stencils, face_mask)


def solution(mesh):
    sizes = dict(mesh.shape)
    return jax.shard_map(
        functools.partial(on_device, sizes["gx"], sizes["gy"]),
        mesh=mesh,
        in_specs=(P("gx", "gy", None), P("gx", "gy", None), P(), P()),
        out_specs=(P("gx", "gy", None), P("gx", "gy", None), P()),
        check_vma=False,
    )
```

```python
import functools

import jax
import jax.numpy as jnp
from jax import lax
from jax.experimental import pallas as pl
from jax.experimental.pallas import tpu as pltpu
from jax.sharding import PartitionSpec as P

MESH = pl.DeviceIdType.MESH
LEVELS = 4
NZ = 128
CHUNK = 384
UNROLL = 8
RIM = (3, 6, 6, 6, 8)
WIDE = 6
KNOWN = ((0, 0), (0, 0), (2, 0), (2, 2), (2, 2))
LESS = (0, 2, 1, 1, 1)
SCALES = tuple(4.0**level for level in range(LEVELS + 1))


def pieces(level, block, axis, rim):
    if level <= 1:
        return [(-1, block - rim, rim), (0, 0, block), (1, 0, rim)]
    if level == 2:
        if axis == 0:
            return [(-1, -2, 4), (0, -2, 8), (1, 2, 4)]
        return [(-1, 2, 6), (0, 0, 8), (1, 0, 6)]
    if level == 3:
        if axis == 0:
            return [(-2, -2, 4), (0, -2, 6), (2, 0, 4)]
        return [(-1, -2, 4), (0, -2, 8), (1, 2, 4)]
    if axis == 0:
        return [(-6, -2, 3), (-3, -2, 3), (0, -2, 5), (3, 0, 3), (6, 0, 3)]
    return [(-3, -2, 2), (-2, -2, 4), (0, -2, 6), (2, 0, 4), (3, 2, 2)]


class Level:
    def __init__(self, level, block, rim):
        self.index = level
        self.rows, self.cols = block
        self.rim = rim
        self.high = self.rows + 2 * self.rim
        self.pitch = self.cols + 2 * self.rim
        self.store = self.high + 1
        while self.store * self.pitch % 8:
            self.store += 1
        known_rows, known_cols = KNOWN[level]
        self.pad_rows, self.pad_cols = known_rows, known_cols
        self.slots = 3 if level == 0 else 2
        self.stage_rows = self.rows + 2 * self.pad_rows
        self.stage_pitch = -(-(self.cols + 2 * self.pad_cols) // 8) * 8
        self.cuts = (pieces(level, self.rows, 0, rim), pieces(level, self.cols, 1, rim))
        received = sum(n for d, s, n in self.cuts[0]) * sum(n for d, s, n in self.cuts[1])
        own = [n for d, s, n in self.cuts[0] if d == 0][0] * [n for d, s, n in self.cuts[1] if d == 0][0]
        assert received == self.high * self.pitch
        self.arriving = received - own

    def span(self, depth):
        return depth * self.pitch + depth, (self.high - depth - 1) * self.pitch + self.pitch - depth


def blocks(first, last, body, chunk=CHUNK):
    count = last - first
    chunk = min(chunk, count)
    steps = -(-count // chunk)
    if steps <= 2:
        for step in range(steps):
            body(min(first + step * chunk, last - chunk), chunk)
        return

    def one(step, carry):
        body(jnp.minimum(first + step * chunk, last - chunk), chunk)
        return carry

    lax.fori_loop(0, steps, one, 0)


def hops_x(offset):
    return min(abs(offset), 8 - abs(offset)) + (offset != 0)


def hops_y(offset):
    return abs(offset) / 2


def lanes(shape):
    return lax.broadcasted_iota(jnp.int32, shape, 1)


def from_below(v):
    return jnp.where(lanes(v.shape) == 0, 0.0, pltpu.roll(v, 1, 1))


def from_above(v):
    return jnp.where(lanes(v.shape) == NZ - 1, 0.0, pltpu.roll(v, NZ - 1, 1))


def stencil_at(src, weight, pitch, row, rows):
    sums = [None, None, None]
    for a in range(3):
        for b in range(3):
            v = src[pl.ds(row + (a - 1) * pitch + b - 1, rows), :]
            for c in range(3):
                term = weight(9 * a + 3 * b + c) * v
                sums[c] = term if sums[c] is None else sums[c] + term
    return sums[1] + from_below(sums[0]) + from_above(sums[2])


def operate_at(src, diag, pitch, row, rows):
    v = src[pl.ds(row, rows), :]
    beside = (src[pl.ds(row - pitch, rows), :] + src[pl.ds(row + pitch, rows), :]) + (
        src[pl.ds(row - 1, rows), :] + src[pl.ds(row + 1, rows), :]
    )
    return diag[pl.ds(row, rows), :] * v - (beside + (from_below(v) + from_above(v)))


def smooth(dst, src, weight, lv, depth, mask=None, add=None):
    def body(row, rows):
        value = stencil_at(src, weight, lv.pitch, row, rows)
        if add is not None:
            value = value + add[pl.ds(row, rows), :]
        if mask is not None:
            value = value * mask[pl.ds(row, rows), :]
        dst[pl.ds(row, rows), :] = value

    blocks(*lv.span(depth), body)


def remain(dst, src, field, diag, mask, lv, depth):
    def body(row, rows):
        value = src[pl.ds(row, rows), :] - operate_at(field, diag, lv.pitch, row, rows)
        dst[pl.ds(row, rows), :] = value * mask[pl.ds(row, rows), :]

    blocks(*lv.span(depth), body)


def restrict(stage, fine, lv, below):
    known_rows, known_cols = KNOWN[below.index]
    first = -known_cols
    starts = range(first, below.cols + known_cols, 8)

    def body(step, carry):
        for start in starts:
            row = (lv.rim + 2 * (step - known_rows)) * lv.pitch + lv.rim + 2 * start
            total = (fine[pl.ds(row, 8, stride=2), :] + fine[pl.ds(row + 1, 8, stride=2), :]) + (
                fine[pl.ds(row + lv.pitch, 8, stride=2), :] + fine[pl.ds(row + lv.pitch + 1, 8, stride=2), :]
            )
            at = (below.pad_rows - known_rows + step) * below.stage_pitch + below.pad_cols + start
            width = min(8, below.cols + known_cols - start)
            stage[pl.ds(at, width), :] = 0.25 * total[:width]
        return carry

    count = below.rows + 2 * known_rows
    if count <= 4:
        for step in range(count):
            body(step, 0)
    else:
        lax.fori_loop(0, count, body, 0)


def prolong_onto(dst, base, coarse, lv, below, half):
    first, last = -half, below.cols + half
    starts = []
    start = first
    while True:
        if last - start <= 8:
            starts.append(max(first, last - 8))
            break
        starts.append(start)
        start += 8

    def body(step, carry):
        line = step - half
        values = [
            coarse[pl.ds((below.rim + line) * below.pitch + below.rim + start, 8), :] for start in starts
        ]
        for part in range(2):
            for start, value in zip(starts, values):
                row = (lv.rim + 2 * line + part) * lv.pitch + lv.rim + 2 * start
                for side in range(2):
                    where = pl.ds(row + side, 8, stride=2)
                    dst[where, :] = base[where, :] + value
        return carry

    count = below.rows + 2 * half
    lax.fori_loop(0, count, body, 0)


def folded(v):
    rows = v.shape[0]
    total = v[0:8]
    for at in range(8, rows, 8):
        total = total + v[at : at + 8]
    return total


def products(cot, cot_first, cot_pitch, field, lv, totals=None):
    width = max(8, lv.cols)
    keep = None
    if lv.cols < 8:
        keep = lax.broadcasted_iota(jnp.int32, (8, NZ), 0) < lv.cols

    def body(step, totals):
        here = cot[pl.ds(cot_first + step * cot_pitch, width), :]
        if keep is not None:
            here = jnp.where(keep, here, 0.0)
        turned = (from_above(here), here, from_below(here))
        out = []
        for a in range(3):
            for b in range(3):
                v = field[pl.ds((lv.rim + step + a - 1) * lv.pitch + lv.rim + b - 1, width), :]
                for c in range(3):
                    out.append(totals[len(out)] + folded(turned[c] * v))
        return tuple(out)

    if totals is None:
        totals = tuple(jnp.zeros((8, NZ), jnp.float32) for _ in range(27))
    if lv.rows <= 2:
        for step in range(lv.rows):
            totals = body(step, totals)
        return totals
    unroll = min(UNROLL, lv.rows)

    def several(step, totals):
        for part in range(unroll):
            totals = body(step * unroll + part, totals)
        return totals

    return lax.fori_loop(0, lv.rows // unroll, several, totals)


def keep_sums(sums, totals, row):
    for entry, total in enumerate(totals):
        sums[pl.ds(row * 32 + entry, 1), :] = jnp.sum(total, axis=0, keepdims=True)


def kernel(gx_size, gy_size, lvs, rhs, target, stencils_in, walls_in, solution_out, grad_out, weights_out, *scratch):
    lvs, wide = lvs[: LEVELS + 1], lvs[LEVELS + 1]
    scratch = list(scratch)
    take = lambda: scratch.pop(0)
    src = [[take() for _ in lvs] for _ in range(2)]
    aft = [[take() for _ in lvs] for _ in range(2)]
    pre = [take() for _ in lvs]
    mid = [take() for _ in lvs]
    out = [take() for _ in lvs]
    mask = [take() for _ in lvs]
    diag = [take() for _ in lvs]
    stage = [take() for _ in lvs]
    last_rest = [take() for _ in range(2)]
    wide_src, wide_pre, wide_mid, wide_aft, wide_out, wide_mask, wide_diag = (take() for _ in range(7))
    goal, grad, sums, mine, over_y, over_x = (take() for _ in range(6))
    stencils, walls = take(), take()
    recv, send, local, io, reduce_send, reduce_recv, extra_send, extra_recv, extra_local = (take() for _ in range(9))

    gx, gy = lax.axis_index("gx"), lax.axis_index("gy")

    def flat(ref, lv):
        return ref.reshape(lv.slots * lv.stage_rows * lv.stage_pitch, NZ)

    stages = [flat(stage[i], lv) for i, lv in enumerate(lvs)]
    blocks3 = [[src[way][i].reshape(lv.store, lv.pitch, NZ) for i, lv in enumerate(lvs)] for way in range(2)]
    grid3 = lambda ref, lv: ref.reshape(lv.store, lv.pitch, NZ)

    def device(x, y):
        return (lax.rem(x + 2 * gx_size, gx_size), lax.rem(y + 2 * gy_size, gy_size))

    barrier = pltpu.get_barrier_semaphore()
    near = [(d, e) for d in (-1, 0, 1) for e in (-1, 0, 1) if (d, e) != (0, 0)]
    for d, e in near:
        pl.semaphore_signal(barrier, inc=1, device_id=device(gx + d, gy + e), device_id_type=MESH)
    load_rhs = pltpu.make_async_copy(rhs, stage[0].at[0], io.at[1])
    load_rhs.start()
    load_walls = pltpu.make_async_copy(walls_in, walls, io.at[4])
    load_walls.start()
    load_stencils = pltpu.make_async_copy(stencils_in, stencils, io.at[5])
    load_stencils.start()
    load_target = pltpu.make_async_copy(target, stage[0].at[1], io.at[0])
    load_target.start()

    def clear(i):
        lv = lvs[i]
        rows = lv.stage_rows * lv.stage_pitch

        def body(row, count):
            stages[i][pl.ds(row, count), :] = jnp.zeros((count, NZ), jnp.float32)

        blocks((lv.slots - 1) * rows, lv.slots * rows, body)

    def lay_out(lv, mask_to, diag_to):
        wall = [walls[k].astype(jnp.float32) for k in range(6)]
        total_rows, total_cols = gx_size * lv.rows, gy_size * lv.cols
        starts = list(range(0, lv.pitch, 8))

        def body(step, carry):
            line = gx * lv.rows - lv.rim + step
            first = jnp.where(line == 0, wall[0], 0.0) + jnp.where(line == total_rows - 1, wall[1], 0.0)
            within = (line >= 0) & (line < total_rows)
            for start in starts:
                column = gy * lv.cols - lv.rim + start + lax.broadcasted_iota(jnp.int32, (8, NZ), 0)
                lane = lanes((8, NZ))
                tally = first + jnp.where(column == 0, wall[2], 0.0) + jnp.where(column == total_cols - 1, wall[3], 0.0)
                tally = tally + jnp.where(lane == 0, wall[4], 0.0) + jnp.where(lane == NZ - 1, wall[5], 0.0)
                inside = (column >= 0) & (column < total_cols) & within
                where = pl.ds(step * lv.pitch + start, 8)
                diag_to[where, :] = 6.0 - tally
                mask_to[where, :] = jnp.where(inside, 1.0, 0.0)
            return carry

        lax.fori_loop(0, lv.high, body, 0)

    def exchange(lv, staged, slot, landing, send_to, recv_to, local_to):
        rows, cols = lv.cuts
        pairs = [(x, y) for x in rows for y in cols]
        pairs.sort(key=lambda pair: -(hops_x(pair[0][0]) + hops_y(pair[1][0])))
        for (dx, first_x, count_x), (dy, first_y, count_y) in pairs:
            to_x, to_y = gx - dx, gy - dy
            window = pl.ds(lv.pad_rows + first_x, count_x), pl.ds(lv.pad_cols + first_y, count_y)
            dst = landing.at[
                pl.ds(lv.rim + dx * lv.rows + first_x, count_x), pl.ds(lv.rim + dy * lv.cols + first_y, count_y)
            ]
            if dx == 0 and dy == 0:
                pltpu.make_async_copy(staged.at[slot, window[0], window[1]], dst, local_to).start()
                continue
            outside = (to_x < 0) | (to_x >= gx_size) | (to_y < 0) | (to_y >= gy_size)
            pltpu.make_async_remote_copy(
                src_ref=staged.at[jnp.where(outside, lv.slots - 1, slot), window[0], window[1]],
                dst_ref=dst,
                send_sem=send_to,
                recv_sem=recv_to,
                device_id=device(to_x, to_y),
                device_id_type=MESH,
            ).start()

    def exchange_level(way, i):
        exchange(lvs[i], stage[i], 0, blocks3[way][i], send.at[way, i], recv.at[way, i], local.at[way, i])

    def await_bytes(ref, rows, sem):
        pltpu.make_async_copy(ref.at[pl.ds(0, rows)], ref.at[pl.ds(0, rows)], sem).wait()

    def arrived(way, i):
        lv = lvs[i]
        await_bytes(src[way][i], lv.arriving, recv.at[way, i])
        await_bytes(src[way][i], lv.high * lv.pitch - lv.arriving, local.at[way, i])

    def sent(way, i):
        await_bytes(src[way][i], lvs[i].arriving, send.at[way, i])

    def weights(way, row):
        if way == 0:
            return lambda entry: stencils[row, entry]
        return lambda entry: stencils[row, 26 - entry]

    def down(way, waiting):
        for i in range(LEVELS):
            lv = lvs[i]
            if i > 0:
                exchange_level(way, i)
            waiting(i)
            if way == 0 or i > 0:
                arrived(way, i)
            depth = 2 if (way, i) == (0, 0) else 1
            smooth(pre[i], src[way][i], weights(way, i if way == 0 else LEVELS + i), lv, depth, mask[i])
            known = max(KNOWN[i + 1])
            remain(mid[i], src[way][i], pre[i], diag[i], mask[i], lv, lv.rim - 2 * known)
            if way == 1:
                sent(0, i + 1)
            restrict(stages[i + 1], mid[i], lv, lvs[i + 1])

    def across(way, waiting):
        lv = lvs[LEVELS]
        less = way * LESS[LEVELS]
        weight = weights(way, 2 * LEVELS)
        exchange_level(way, LEVELS)
        waiting(LEVELS)
        arrived(way, LEVELS)
        b = src[way][LEVELS]
        x, y = pre[LEVELS], mid[LEVELS]
        rest = (aft[way][LEVELS], last_rest[way])
        inside, center = mask[LEVELS], diag[LEVELS]
        smooth(x, b, weight, lv, 1 + less, inside)
        remain(rest[0], b, x, center, inside, lv, 2 + less)
        smooth(y, rest[0], weight, lv, 3 + less, inside, x)
        remain(rest[1], b, y, center, inside, lv, 4 + less)
        smooth(out[LEVELS], rest[1], weight, lv, 5 + less, inside, y)

    def up(way):
        for i in reversed(range(1, LEVELS)):
            lv = lvs[i]
            less = way * LESS[i]
            prolong_onto(mid[i], pre[i], out[i + 1], lv, lvs[i + 1], 3 - way)
            remain(aft[way][i], src[way][i], mid[i], diag[i], mask[i], lv, 2 + less)
            weight = weights(way, LEVELS + i if way == 0 else i)
            smooth(out[i], aft[way][i], weight, lv, 3 + less, mask[i], mid[i])

    fine = lvs[0]
    load_walls.wait()
    lay_out(fine, mask[0], diag[0])
    clear(0)
    load_stencils.wait()
    load_rhs.wait()
    pl.semaphore_wait(barrier, len(near))
    exchange_level(0, 0)
    load_target.wait()
    exchange(wide, stage[0], 0, grid3(wide_src, wide), extra_send.at[0], extra_recv.at[0], extra_local.at[0])
    exchange(fine, stage[0], 1, grid3(goal, fine), extra_send.at[1], extra_recv.at[1], extra_local.at[1])

    def forward_waits(i):
        if i == 0:
            sums[...] = jnp.zeros(sums.shape, jnp.float32)
            for level in range(1, LEVELS + 1):
                clear(level)
                lay_out(lvs[level], mask[level], diag[level])
        if i == 1:
            lay_out(wide, wide_mask, wide_diag)
        if i == 2:
            await_bytes(wide_src, wide.arriving, extra_recv.at[0])
            await_bytes(wide_src, wide.high * wide.pitch - wide.arriving, extra_local.at[0])
            smooth(wide_pre, wide_src, weights(0, 0), wide, 1, wide_mask)
        if i == LEVELS:
            await_bytes(goal, fine.arriving, extra_recv.at[1])
            await_bytes(goal, fine.high * fine.pitch - fine.arriving, extra_local.at[1])
            await_bytes(wide_src, wide.arriving, extra_send.at[0])
            await_bytes(goal, fine.arriving, extra_send.at[1])
            sent(0, 0)

    down(0, forward_waits)
    across(0, forward_waits)
    up(0)
    prolong_onto(wide_mid, wide_pre, out[1], wide, lvs[1], 3)
    remain(wide_aft, wide_src, wide_mid, wide_diag, wide_mask, wide, 2)
    smooth(wide_out, wide_aft, weights(0, LEVELS), wide, 3, wide_mask, wide_mid)

    pitch8 = -(-fine.pitch // 8) * 8
    inset = wide.rim - fine.rim

    def error_at(step, carry):
        for part in range(fine.high // 2):
            line = step * (fine.high // 2) + part
            where = pl.ds(line * fine.pitch, pitch8)
            src[1][0][where, :] = wide_out[pl.ds((line + inset) * wide.pitch + inset, pitch8), :] - goal[where, :]
        return carry

    lax.fori_loop(0, 2, error_at, 0)
    own_solution = grid3(wide_out, wide).at[pl.ds(wide.rim, fine.rows), pl.ds(wide.rim, fine.cols)]
    save_solution = pltpu.make_async_copy(own_solution, solution_out, io.at[2])
    save_solution.start()

    def post_sums(i):
        field = aft[0][i] if i else wide_aft
        lv = lvs[i] if i else wide
        if i:
            cot, first, pitch = stages[i], lvs[i].pad_rows * lvs[i].stage_pitch + lvs[i].pad_cols, lvs[i].stage_pitch
        else:
            cot, first, pitch = src[1][0], fine.rim * fine.pitch + fine.rim, fine.pitch
        keep_sums(sums, products(cot, first, pitch, field, lv), LEVELS + i)

    def backward_waits(i):
        if i == 1:
            post_sums(0)
        if 1 <= i < LEVELS:
            post_sums(i)

    down(1, backward_waits)
    across(1, backward_waits)
    up(1)
    prolong_onto(mid[0], pre[0], out[1], fine, lvs[1], 1)
    remain(aft[1][0], src[1][0], mid[0], diag[0], mask[0], fine, 2)

    bottom = lvs[LEVELS]
    at = bottom.rim * bottom.pitch + bottom.rim
    totals = products(src[1][LEVELS], at, bottom.pitch, last_rest[0], bottom)
    totals = products(aft[1][LEVELS], at, bottom.pitch, aft[0][LEVELS], bottom, totals)
    totals = products(last_rest[1], at, bottom.pitch, src[0][LEVELS], bottom, totals)
    keep_sums(sums, totals, 2 * LEVELS)
    for i in reversed(range(LEVELS)):
        lv = lvs[i]
        at = lv.rim * lv.pitch + lv.rim
        keep_sums(sums, products(aft[1][i], at, lv.pitch, src[0][i], lv), i)

    ones = jnp.ones((8, NZ), jnp.float32)
    for part in range(3):
        line = lax.dot_general(
            ones,
            sums[pl.ds(part * NZ, NZ), :],
            (((1,), (1,)), ((), ())),
            precision=lax.Precision.HIGHEST,
            preferred_element_type=jnp.float32,
        )
        mine[0, pl.ds(part, 1), :] = line[0:1]

    def spread(slot, held, me, order, where):
        source = mine.at[slot, pl.ds(0, 3)]
        for step in order:
            pltpu.make_async_remote_copy(
                src_ref=source,
                dst_ref=held.at[me, pl.ds(0, 3)],
                send_sem=reduce_send.at[slot],
                recv_sem=reduce_recv.at[slot],
                device_id=where(step),
                device_id_type=MESH,
            ).start()
        held[me] = mine[slot]

    def gathered(slot, held, size):
        await_bytes(src[0][0], 3 * (size - 1), reduce_recv.at[slot])
        total = held[0]
        for step in range(1, size):
            total = total + held[step]
        return total

    order = sorted(range(1, gy_size), key=lambda step: -min(step, gy_size - step))
    spread(0, over_y, gy, order, lambda step: device(gx, gy + step))

    def grad_at(step, carry):
        for part in range(UNROLL):
            line = step * UNROLL + part
            row = (fine.rim + line) * fine.pitch + fine.rim
            value = stencil_at(aft[1][0], weights(1, 0), fine.pitch, row, fine.cols)
            grad[line] = value + mid[0][pl.ds(row, fine.cols), :]
        return carry

    lax.fori_loop(0, fine.rows // UNROLL, grad_at, 0)
    save_grad = pltpu.make_async_copy(grad, grad_out, io.at[3])
    save_grad.start()

    mine[1] = gathered(0, over_y, gy_size)
    order = sorted(range(1, gx_size), key=lambda step: -min(step % 8, 8 - step % 8) - min(step, gx_size - step) / 8)
    spread(1, over_x, gx, order, lambda step: device(gx + step, gy))
    await_bytes(src[0][0], 3 * (gy_size - 1), reduce_send.at[0])
    for i in range(1, LEVELS + 1):
        sent(1, i)
    save_solution.wait()
    save_grad.wait()
    total = gathered(1, over_x, gx_size)
    await_bytes(src[0][0], 3 * (gx_size - 1), reduce_send.at[1])
    cells = gx_size * lvs[0].rows * gy_size * lvs[0].cols * NZ
    for row in range(2 * LEVELS + 1):
        scale = SCALES[row % LEVELS if row < 2 * LEVELS else LEVELS] / cells
        part, lane = row // 4, 32 * (row % 4)
        weights_out[pl.ds(row, 1), :] = total[part : part + 1, lane : lane + 27] * scale


def put_out(*refs):
    sems = refs[6]
    copies = [pltpu.make_async_copy(refs[i], refs[3 + i], sems.at[i]) for i in range(3)]
    for copy in copies:
        copy.start()
    for copy in copies:
        copy.wait()


def on_device(gx_size, gy_size, rhs, target, stencils, face_mask):
    rows, cols, _ = rhs.shape
    lvs = [Level(i, (rows >> i, cols >> i), RIM[i]) for i in range(LEVELS + 1)]
    wide = Level(0, (rows, cols), WIDE)
    field = lambda lv: pltpu.VMEM((lv.store * lv.pitch, NZ), jnp.float32)
    scratch = []
    for _ in range(9):
        scratch += [field(lv) for lv in lvs]
    scratch += [pltpu.VMEM((lv.slots, lv.stage_rows, lv.stage_pitch, NZ), jnp.float32) for lv in lvs]
    scratch += [field(lvs[LEVELS])] * 2
    scratch += [field(wide)] * 7
    scratch += [field(lvs[0]), pltpu.VMEM((rows, cols, NZ), jnp.float32)]
    scratch += [
        pltpu.VMEM((3 * NZ, NZ), jnp.float32),
        pltpu.VMEM((2, 8, NZ), jnp.float32),
        pltpu.VMEM((gy_size, 8, NZ), jnp.float32),
        pltpu.VMEM((gx_size, 8, NZ), jnp.float32),
        pltpu.SMEM(stencils.shape, jnp.float32),
        pltpu.SMEM(face_mask.shape, jnp.int32),
        pltpu.SemaphoreType.DMA((2, LEVELS + 1)),
        pltpu.SemaphoreType.DMA((2, LEVELS + 1)),
        pltpu.SemaphoreType.DMA((2, LEVELS + 1)),
        pltpu.SemaphoreType.DMA((6,)),
        pltpu.SemaphoreType.DMA((2,)),
        pltpu.SemaphoreType.DMA((2,)),
        pltpu.SemaphoreType.DMA((2,)),
        pltpu.SemaphoreType.DMA((2,)),
        pltpu.SemaphoreType.DMA((2,)),
    ]
    results = pl.pallas_call(
        functools.partial(kernel, gx_size, gy_size, lvs + [wide]),
        out_shape=(
            jax.ShapeDtypeStruct(rhs.shape, jnp.float32),
            jax.ShapeDtypeStruct(rhs.shape, jnp.float32),
            jax.ShapeDtypeStruct(stencils.shape, jnp.float32),
        ),
        in_specs=[
            pl.BlockSpec(memory_space=pltpu.HBM),
            pl.BlockSpec(memory_space=pltpu.HBM),
            pl.BlockSpec(memory_space=pltpu.HBM),
            pl.BlockSpec(memory_space=pltpu.HBM),
        ],
        out_specs=(
            pl.BlockSpec(memory_space=pl.ANY),
            pl.BlockSpec(memory_space=pl.ANY),
            pl.BlockSpec(memory_space=pltpu.VMEM),
        ),
        scratch_shapes=scratch,
        compiler_params=pltpu.CompilerParams(
            collective_id=0, has_side_effects=True, vmem_limit_bytes=60 << 20
        ),
        cost_estimate=pl.CostEstimate(flops=60_000_000, bytes_accessed=1_100_000, transcendentals=0),
    )(rhs, target, stencils, face_mask)
    return pl.pallas_call(
        put_out,
        out_shape=tuple(jax.ShapeDtypeStruct(r.shape, r.dtype) for r in results),
        in_specs=[pl.BlockSpec(memory_space=pl.ANY)] * 3,
        out_specs=(pl.BlockSpec(memory_space=pl.ANY),) * 3,
        scratch_shapes=[pltpu.SemaphoreType.DMA((3,))],
        compiler_params=pltpu.CompilerParams(vmem_limit_bytes=60 << 20),
    )(*results)


def solution(mesh):
    sizes = dict(mesh.shape)
    return jax.shard_map(
        functools.partial(on_device, sizes["gx"], sizes["gy"]),
        mesh=mesh,
        in_specs=(P("gx", "gy", None), P("gx", "gy", None), P(), P()),
        out_specs=(P("gx", "gy", None), P("gx", "gy", None), P()),
        check_vma=False,
    )
```

```python
import functools

import jax
import jax.numpy as jnp
from jax import lax
from jax.experimental import pallas as pl
from jax.experimental.pallas import tpu as pltpu
from jax.sharding import PartitionSpec as P

MESH = pl.DeviceIdType.MESH
LEVELS = 4
NZ = 128
CHUNK = 384
UNROLL = 8
RIM = (3, 6, 6, 6, 8)
WIDE = 6
KNOWN = ((0, 0), (0, 0), (2, 0), (2, 2), (2, 2))
LESS = (0, 2, 1, 1, 1)
SCALES = tuple(4.0**level for level in range(LEVELS + 1))


def pieces(level, block, axis, rim):
    if level <= 1:
        return [(-1, block - rim, rim), (0, 0, block), (1, 0, rim)]
    if level == 2:
        if axis == 0:
            return [(-1, -2, 4), (0, -2, 8), (1, 2, 4)]
        return [(-1, 2, 6), (0, 0, 8), (1, 0, 6)]
    if level == 3:
        if axis == 0:
            return [(-2, -2, 4), (0, -2, 6), (2, 0, 4)]
        return [(-1, -2, 4), (0, -2, 8), (1, 2, 4)]
    if axis == 0:
        return [(-6, -2, 3), (-3, -2, 3), (0, -2, 5), (3, 0, 3), (6, 0, 3)]
    return [(-3, -2, 2), (-2, -2, 4), (0, -2, 6), (2, 0, 4), (3, 2, 2)]


class Level:
    def __init__(self, level, block, rim):
        self.index = level
        self.rows, self.cols = block
        self.rim = rim
        self.high = self.rows + 2 * self.rim
        self.pitch = self.cols + 2 * self.rim
        self.store = self.high + 1
        while self.store * self.pitch % 8:
            self.store += 1
        known_rows, known_cols = KNOWN[level]
        self.pad_rows, self.pad_cols = known_rows, known_cols
        self.slots = 3 if level == 0 else 2
        self.stage_rows = self.rows + 2 * self.pad_rows
        self.stage_pitch = -(-(self.cols + 2 * self.pad_cols) // 8) * 8
        self.cuts = (pieces(level, self.rows, 0, rim), pieces(level, self.cols, 1, rim))
        received = sum(n for d, s, n in self.cuts[0]) * sum(n for d, s, n in self.cuts[1])
        own = [n for d, s, n in self.cuts[0] if d == 0][0] * [n for d, s, n in self.cuts[1] if d == 0][0]
        assert received == self.high * self.pitch
        self.arriving = received - own

    def span(self, depth):
        return depth * self.pitch + depth, (self.high - depth - 1) * self.pitch + self.pitch - depth


def blocks(first, last, body, chunk=CHUNK):
    count = last - first
    chunk = min(chunk, count)
    steps = -(-count // chunk)
    if steps <= 2:
        for step in range(steps):
            body(min(first + step * chunk, last - chunk), chunk)
        return

    def one(step, carry):
        body(jnp.minimum(first + step * chunk, last - chunk), chunk)
        return carry

    lax.fori_loop(0, steps, one, 0)


def hops_x(offset):
    return min(abs(offset), 8 - abs(offset)) + (offset != 0)


def hops_y(offset):
    return abs(offset) / 2


def lanes(shape):
    return lax.broadcasted_iota(jnp.int32, shape, 1)


def from_below(v):
    return jnp.where(lanes(v.shape) == 0, 0.0, pltpu.roll(v, 1, 1))


def from_above(v):
    return jnp.where(lanes(v.shape) == NZ - 1, 0.0, pltpu.roll(v, NZ - 1, 1))


def stencil_at(src, weight, pitch, row, rows):
    sums = [None, None, None]
    for a in range(3):
        for b in range(3):
            v = src[pl.ds(row + (a - 1) * pitch + b - 1, rows), :]
            for c in range(3):
                term = weight(9 * a + 3 * b + c) * v
                sums[c] = term if sums[c] is None else sums[c] + term
    return sums[1] + from_below(sums[0]) + from_above(sums[2])


def operate_at(src, diag, pitch, row, rows):
    v = src[pl.ds(row, rows), :]
    beside = (src[pl.ds(row - pitch, rows), :] + src[pl.ds(row + pitch, rows), :]) + (
        src[pl.ds(row - 1, rows), :] + src[pl.ds(row + 1, rows), :]
    )
    return diag[pl.ds(row, rows), :] * v - (beside + (from_below(v) + from_above(v)))


def smooth(dst, src, weight, lv, depth, mask=None, add=None):
    def body(row, rows):
        value = stencil_at(src, weight, lv.pitch, row, rows)
        if add is not None:
            value = value + add[pl.ds(row, rows), :]
        if mask is not None:
            value = value * mask[pl.ds(row, rows), :]
        dst[pl.ds(row, rows), :] = value

    blocks(*lv.span(depth), body)


def remain(dst, src, field, diag, mask, lv, depth):
    def body(row, rows):
        value = src[pl.ds(row, rows), :] - operate_at(field, diag, lv.pitch, row, rows)
        dst[pl.ds(row, rows), :] = value * mask[pl.ds(row, rows), :]

    blocks(*lv.span(depth), body)


def restrict(stage, fine, lv, below):
    known_rows, known_cols = KNOWN[below.index]
    first = -known_cols
    starts = range(first, below.cols + known_cols, 8)

    def body(step, carry):
        for start in starts:
            row = (lv.rim + 2 * (step - known_rows)) * lv.pitch + lv.rim + 2 * start
            total = (fine[pl.ds(row, 8, stride=2), :] + fine[pl.ds(row + 1, 8, stride=2), :]) + (
                fine[pl.ds(row + lv.pitch, 8, stride=2), :] + fine[pl.ds(row + lv.pitch + 1, 8, stride=2), :]
            )
            at = (below.pad_rows - known_rows + step) * below.stage_pitch + below.pad_cols + start
            width = min(8, below.cols + known_cols - start)
            stage[pl.ds(at, width), :] = 0.25 * total[:width]
        return carry

    count = below.rows + 2 * known_rows
    for step in range(count):
        body(step, 0)


def prolong_onto(dst, base, coarse, lv, below, half):
    first, last = -half, below.cols + half
    starts = []
    start = first
    while True:
        if last - start <= 8:
            starts.append(max(first, last - 8))
            break
        starts.append(start)
        start += 8

    def body(step, carry):
        line = step - half
        values = [
            coarse[pl.ds((below.rim + line) * below.pitch + below.rim + start, 8), :] for start in starts
        ]
        for part in range(2):
            for start, value in zip(starts, values):
                row = (lv.rim + 2 * line + part) * lv.pitch + lv.rim + 2 * start
                for side in range(2):
                    where = pl.ds(row + side, 8, stride=2)
                    dst[where, :] = base[where, :] + value
        return carry

    for step in range(below.rows + 2 * half):
        body(step, 0)


def folded(v):
    rows = v.shape[0]
    total = v[0:8]
    for at in range(8, rows, 8):
        total = total + v[at : at + 8]
    return total


def products(cot, cot_first, cot_pitch, field, lv, totals=None):
    width = max(8, lv.cols)
    keep = None
    if lv.cols < 8:
        keep = lax.broadcasted_iota(jnp.int32, (8, NZ), 0) < lv.cols

    def body(step, totals):
        here = cot[pl.ds(cot_first + step * cot_pitch, width), :]
        if keep is not None:
            here = jnp.where(keep, here, 0.0)
        turned = (from_above(here), here, from_below(here))
        out = []
        for a in range(3):
            for b in range(3):
                v = field[pl.ds((lv.rim + step + a - 1) * lv.pitch + lv.rim + b - 1, width), :]
                for c in range(3):
                    out.append(totals[len(out)] + folded(turned[c] * v))
        return tuple(out)

    if totals is None:
        totals = tuple(jnp.zeros((8, NZ), jnp.float32) for _ in range(27))
    if lv.rows <= 2:
        for step in range(lv.rows):
            totals = body(step, totals)
        return totals
    unroll = min(UNROLL, lv.rows)

    def several(step, totals):
        for part in range(unroll):
            totals = body(step * unroll + part, totals)
        return totals

    return lax.fori_loop(0, lv.rows // unroll, several, totals)


def keep_sums(sums, totals, row):
    for entry, total in enumerate(totals):
        sums[pl.ds(row * 32 + entry, 1), :] = jnp.sum(total, axis=0, keepdims=True)


def kernel(gx_size, gy_size, lvs, rhs, target, stencils_in, walls_in, solution_out, grad_out, weights_out, *scratch):
    lvs, wide = lvs[: LEVELS + 1], lvs[LEVELS + 1]
    scratch = list(scratch)
    take = lambda: scratch.pop(0)
    src = [[take() for _ in lvs] for _ in range(2)]
    aft = [[take() for _ in lvs] for _ in range(2)]
    pre = [take() for _ in lvs]
    mid = [take() for _ in lvs]
    out = [take() for _ in lvs]
    mask = [take() for _ in lvs]
    diag = [take() for _ in lvs]
    stage = [take() for _ in lvs]
    last_rest = [take() for _ in range(2)]
    wide_src, wide_pre, wide_mid, wide_aft, wide_out, wide_mask, wide_diag = (take() for _ in range(7))
    goal, grad, sums, mine, over_y, over_x = (take() for _ in range(6))
    stencils, walls = take(), take()
    recv, send, local, io, reduce_send, reduce_recv, extra_send, extra_recv, extra_local = (take() for _ in range(9))

    gx, gy = lax.axis_index("gx"), lax.axis_index("gy")

    def flat(ref, lv):
        return ref.reshape(lv.slots * lv.stage_rows * lv.stage_pitch, NZ)

    stages = [flat(stage[i], lv) for i, lv in enumerate(lvs)]
    blocks3 = [[src[way][i].reshape(lv.store, lv.pitch, NZ) for i, lv in enumerate(lvs)] for way in range(2)]
    grid3 = lambda ref, lv: ref.reshape(lv.store, lv.pitch, NZ)

    def device(x, y):
        return (lax.rem(x + 2 * gx_size, gx_size), lax.rem(y + 2 * gy_size, gy_size))

    barrier = pltpu.get_barrier_semaphore()
    near = [(d, e) for d in (-1, 0, 1) for e in (-1, 0, 1) if (d, e) != (0, 0)]
    for d, e in near:
        pl.semaphore_signal(barrier, inc=1, device_id=device(gx + d, gy + e), device_id_type=MESH)
    load_rhs = pltpu.make_async_copy(rhs, stage[0].at[0], io.at[1])
    load_rhs.start()
    load_walls = pltpu.make_async_copy(walls_in, walls, io.at[4])
    load_walls.start()
    load_stencils = pltpu.make_async_copy(stencils_in, stencils, io.at[5])
    load_stencils.start()
    load_target = pltpu.make_async_copy(target, stage[0].at[1], io.at[0])
    load_target.start()

    def clear(i):
        lv = lvs[i]
        rows = lv.stage_rows * lv.stage_pitch

        def body(row, count):
            stages[i][pl.ds(row, count), :] = jnp.zeros((count, NZ), jnp.float32)

        blocks((lv.slots - 1) * rows, lv.slots * rows, body)

    def lay_out(lv, mask_to, diag_to):
        wall = [walls[k].astype(jnp.float32) for k in range(6)]
        total_rows, total_cols = gx_size * lv.rows, gy_size * lv.cols
        starts = list(range(0, lv.pitch, 8))

        def body(step, carry):
            line = gx * lv.rows - lv.rim + step
            first = jnp.where(line == 0, wall[0], 0.0) + jnp.where(line == total_rows - 1, wall[1], 0.0)
            within = (line >= 0) & (line < total_rows)
            for start in starts:
                column = gy * lv.cols - lv.rim + start + lax.broadcasted_iota(jnp.int32, (8, NZ), 0)
                lane = lanes((8, NZ))
                tally = first + jnp.where(column == 0, wall[2], 0.0) + jnp.where(column == total_cols - 1, wall[3], 0.0)
                tally = tally + jnp.where(lane == 0, wall[4], 0.0) + jnp.where(lane == NZ - 1, wall[5], 0.0)
                inside = (column >= 0) & (column < total_cols) & within
                where = pl.ds(step * lv.pitch + start, 8)
                diag_to[where, :] = 6.0 - tally
                mask_to[where, :] = jnp.where(inside, 1.0, 0.0)
            return carry

        lax.fori_loop(0, lv.high, body, 0)

    def exchange(lv, staged, slot, landing, send_to, recv_to, local_to):
        rows, cols = lv.cuts
        pairs = [(x, y) for x in rows for y in cols]
        pairs.sort(key=lambda pair: -(hops_x(pair[0][0]) + hops_y(pair[1][0])))
        for (dx, first_x, count_x), (dy, first_y, count_y) in pairs:
            to_x, to_y = gx - dx, gy - dy
            window = pl.ds(lv.pad_rows + first_x, count_x), pl.ds(lv.pad_cols + first_y, count_y)
            dst = landing.at[
                pl.ds(lv.rim + dx * lv.rows + first_x, count_x), pl.ds(lv.rim + dy * lv.cols + first_y, count_y)
            ]
            if dx == 0 and dy == 0:
                pltpu.make_async_copy(staged.at[slot, window[0], window[1]], dst, local_to).start()
                continue
            outside = (to_x < 0) | (to_x >= gx_size) | (to_y < 0) | (to_y >= gy_size)
            pltpu.make_async_remote_copy(
                src_ref=staged.at[jnp.where(outside, lv.slots - 1, slot), window[0], window[1]],
                dst_ref=dst,
                send_sem=send_to,
                recv_sem=recv_to,
                device_id=device(to_x, to_y),
                device_id_type=MESH,
            ).start()

    def exchange_level(way, i):
        exchange(lvs[i], stage[i], 0, blocks3[way][i], send.at[way, i], recv.at[way, i], local.at[way, i])

    def await_bytes(ref, rows, sem):
        pltpu.make_async_copy(ref.at[pl.ds(0, rows)], ref.at[pl.ds(0, rows)], sem).wait()

    def arrived(way, i):
        lv = lvs[i]
        await_bytes(src[way][i], lv.arriving, recv.at[way, i])
        await_bytes(src[way][i], lv.high * lv.pitch - lv.arriving, local.at[way, i])

    def sent(way, i):
        await_bytes(src[way][i], lvs[i].arriving, send.at[way, i])

    def weights(way, row):
        if way == 0:
            return lambda entry: stencils[row, entry]
        return lambda entry: stencils[row, 26 - entry]

    def down(way, waiting):
        for i in range(LEVELS):
            lv = lvs[i]
            if i > 0:
                exchange_level(way, i)
            waiting(i)
            if way == 0 or i > 0:
                arrived(way, i)
            depth = 2 if (way, i) == (0, 0) else 1
            smooth(pre[i], src[way][i], weights(way, i if way == 0 else LEVELS + i), lv, depth, mask[i])
            known = max(KNOWN[i + 1])
            remain(mid[i], src[way][i], pre[i], diag[i], mask[i], lv, lv.rim - 2 * known)
            if way == 1:
                sent(0, i + 1)
            restrict(stages[i + 1], mid[i], lv, lvs[i + 1])

    def across(way, waiting):
        lv = lvs[LEVELS]
        less = way * LESS[LEVELS]
        weight = weights(way, 2 * LEVELS)
        exchange_level(way, LEVELS)
        waiting(LEVELS)
        arrived(way, LEVELS)
        b = src[way][LEVELS]
        x, y = pre[LEVELS], mid[LEVELS]
        rest = (aft[way][LEVELS], last_rest[way])
        inside, center = mask[LEVELS], diag[LEVELS]
        smooth(x, b, weight, lv, 1 + less, inside)
        remain(rest[0], b, x, center, inside, lv, 2 + less)
        smooth(y, rest[0], weight, lv, 3 + less, inside, x)
        remain(rest[1], b, y, center, inside, lv, 4 + less)
        smooth(out[LEVELS], rest[1], weight, lv, 5 + less, inside, y)

    def up(way):
        for i in reversed(range(1, LEVELS)):
            lv = lvs[i]
            less = way * LESS[i]
            prolong_onto(mid[i], pre[i], out[i + 1], lv, lvs[i + 1], 3 - way)
            remain(aft[way][i], src[way][i], mid[i], diag[i], mask[i], lv, 2 + less)
            weight = weights(way, LEVELS + i if way == 0 else i)
            smooth(out[i], aft[way][i], weight, lv, 3 + less, mask[i], mid[i])

    fine = lvs[0]
    clear(0)
    load_rhs.wait()
    pl.semaphore_wait(barrier, len(near))
    exchange_level(0, 0)
    load_walls.wait()
    load_stencils.wait()
    lay_out(fine, mask[0], diag[0])
    load_target.wait()
    def forward_waits(i):
        if i == 0:
            sums[...] = jnp.zeros(sums.shape, jnp.float32)
            for level in range(1, LEVELS + 1):
                clear(level)
                lay_out(lvs[level], mask[level], diag[level])
        if i == 1:
            exchange(wide, stage[0], 0, grid3(wide_src, wide), extra_send.at[0], extra_recv.at[0], extra_local.at[0])
            lay_out(wide, wide_mask, wide_diag)
        if i == 2:
            exchange(fine, stage[0], 1, grid3(goal, fine), extra_send.at[1], extra_recv.at[1], extra_local.at[1])
        if i == 3:
            await_bytes(wide_src, wide.arriving, extra_recv.at[0])
            await_bytes(wide_src, wide.high * wide.pitch - wide.arriving, extra_local.at[0])
            smooth(wide_pre, wide_src, weights(0, 0), wide, 1, wide_mask)
        if i == LEVELS:
            await_bytes(goal, fine.arriving, extra_recv.at[1])
            await_bytes(goal, fine.high * fine.pitch - fine.arriving, extra_local.at[1])
            await_bytes(wide_src, wide.arriving, extra_send.at[0])
            await_bytes(goal, fine.arriving, extra_send.at[1])
            sent(0, 0)

    down(0, forward_waits)
    across(0, forward_waits)
    up(0)
    prolong_onto(wide_mid, wide_pre, out[1], wide, lvs[1], 3)
    remain(wide_aft, wide_src, wide_mid, wide_diag, wide_mask, wide, 2)
    smooth(wide_out, wide_aft, weights(0, LEVELS), wide, 3, wide_mask, wide_mid)

    pitch8 = -(-fine.pitch // 8) * 8
    inset = wide.rim - fine.rim

    def error_at(step, carry):
        for part in range(fine.high // 2):
            line = step * (fine.high // 2) + part
            where = pl.ds(line * fine.pitch, pitch8)
            src[1][0][where, :] = wide_out[pl.ds((line + inset) * wide.pitch + inset, pitch8), :] - goal[where, :]
        return carry

    lax.fori_loop(0, 2, error_at, 0)
    own_solution = grid3(wide_out, wide).at[pl.ds(wide.rim, fine.rows), pl.ds(wide.rim, fine.cols)]
    save_solution = pltpu.make_async_copy(own_solution, solution_out, io.at[2])
    save_solution.start()

    def post_sums(i):
        field = aft[0][i] if i else wide_aft
        lv = lvs[i] if i else wide
        if i:
            cot, first, pitch = stages[i], lvs[i].pad_rows * lvs[i].stage_pitch + lvs[i].pad_cols, lvs[i].stage_pitch
        else:
            cot, first, pitch = src[1][0], fine.rim * fine.pitch + fine.rim, fine.pitch
        keep_sums(sums, products(cot, first, pitch, field, lv), LEVELS + i)

    def backward_waits(i):
        if i == 1:
            post_sums(0)
        if 1 <= i < LEVELS:
            post_sums(i)

    down(1, backward_waits)
    across(1, backward_waits)
    up(1)
    prolong_onto(mid[0], pre[0], out[1], fine, lvs[1], 1)
    remain(aft[1][0], src[1][0], mid[0], diag[0], mask[0], fine, 2)

    bottom = lvs[LEVELS]
    at = bottom.rim * bottom.pitch + bottom.rim
    totals = products(src[1][LEVELS], at, bottom.pitch, last_rest[0], bottom)
    totals = products(aft[1][LEVELS], at, bottom.pitch, aft[0][LEVELS], bottom, totals)
    totals = products(last_rest[1], at, bottom.pitch, src[0][LEVELS], bottom, totals)
    keep_sums(sums, totals, 2 * LEVELS)
    for i in reversed(range(LEVELS)):
        lv = lvs[i]
        at = lv.rim * lv.pitch + lv.rim
        keep_sums(sums, products(aft[1][i], at, lv.pitch, src[0][i], lv), i)

    ones = jnp.ones((8, NZ), jnp.float32)
    for part in range(3):
        line = lax.dot_general(
            ones,
            sums[pl.ds(part * NZ, NZ), :],
            (((1,), (1,)), ((), ())),
            precision=lax.Precision.HIGHEST,
            preferred_element_type=jnp.float32,
        )
        mine[0, pl.ds(part, 1), :] = line[0:1]

    def spread(slot, held, me, order, where):
        source = mine.at[slot, pl.ds(0, 3)]
        for step in order:
            pltpu.make_async_remote_copy(
                src_ref=source,
                dst_ref=held.at[me, pl.ds(0, 3)],
                send_sem=reduce_send.at[slot],
                recv_sem=reduce_recv.at[slot],
                device_id=where(step),
                device_id_type=MESH,
            ).start()
        held[me] = mine[slot]

    def gathered(slot, held, size):
        await_bytes(src[0][0], 3 * (size - 1), reduce_recv.at[slot])
        total = held[0]
        for step in range(1, size):
            total = total + held[step]
        return total

    order = sorted(range(1, gy_size), key=lambda step: -min(step, gy_size - step))
    spread(0, over_y, gy, order, lambda step: device(gx, gy + step))

    def grad_at(step, carry):
        for part in range(UNROLL):
            line = step * UNROLL + part
            row = (fine.rim + line) * fine.pitch + fine.rim
            value = stencil_at(aft[1][0], weights(1, 0), fine.pitch, row, fine.cols)
            grad[line] = value + mid[0][pl.ds(row, fine.cols), :]
        return carry

    lax.fori_loop(0, fine.rows // UNROLL, grad_at, 0)
    save_grad = pltpu.make_async_copy(grad, grad_out, io.at[3])
    save_grad.start()

    mine[1] = gathered(0, over_y, gy_size)
    order = sorted(range(1, gx_size), key=lambda step: -min(step % 8, 8 - step % 8) - min(step, gx_size - step) / 8)
    spread(1, over_x, gx, order, lambda step: device(gx + step, gy))
    await_bytes(src[0][0], 3 * (gy_size - 1), reduce_send.at[0])
    for i in range(1, LEVELS + 1):
        sent(1, i)
    save_solution.wait()
    save_grad.wait()
    total = gathered(1, over_x, gx_size)
    await_bytes(src[0][0], 3 * (gx_size - 1), reduce_send.at[1])
    cells = gx_size * lvs[0].rows * gy_size * lvs[0].cols * NZ
    for row in range(2 * LEVELS + 1):
        scale = SCALES[row % LEVELS if row < 2 * LEVELS else LEVELS] / cells
        part, lane = row // 4, 32 * (row % 4)
        weights_out[pl.ds(row, 1), :] = total[part : part + 1, lane : lane + 27] * scale


def put_out(*refs):
    sources, targets, held, sems = refs[:3], refs[3:6], refs[6:9], refs[9]
    loads = [pltpu.make_async_copy(sources[i], held[i], sems.at[0, i]) for i in range(3)]
    stores = [pltpu.make_async_copy(held[i], targets[i], sems.at[1, i]) for i in range(3)]
    for load in loads:
        load.start()
    for load, store in zip(loads, stores):
        load.wait()
        store.start()
    for store in stores:
        store.wait()


def on_device(gx_size, gy_size, rhs, target, stencils, face_mask):
    rows, cols, _ = rhs.shape
    lvs = [Level(i, (rows >> i, cols >> i), RIM[i]) for i in range(LEVELS + 1)]
    wide = Level(0, (rows, cols), WIDE)
    field = lambda lv: pltpu.VMEM((lv.store * lv.pitch, NZ), jnp.float32)
    scratch = []
    for _ in range(9):
        scratch += [field(lv) for lv in lvs]
    scratch += [pltpu.VMEM((lv.slots, lv.stage_rows, lv.stage_pitch, NZ), jnp.float32) for lv in lvs]
    scratch += [field(lvs[LEVELS])] * 2
    scratch += [field(wide)] * 7
    scratch += [field(lvs[0]), pltpu.VMEM((rows, cols, NZ), jnp.float32)]
    scratch += [
        pltpu.VMEM((3 * NZ, NZ), jnp.float32),
        pltpu.VMEM((2, 8, NZ), jnp.float32),
        pltpu.VMEM((gy_size, 8, NZ), jnp.float32),
        pltpu.VMEM((gx_size, 8, NZ), jnp.float32),
        pltpu.SMEM(stencils.shape, jnp.float32),
        pltpu.SMEM(face_mask.shape, jnp.int32),
        pltpu.SemaphoreType.DMA((2, LEVELS + 1)),
        pltpu.SemaphoreType.DMA((2, LEVELS + 1)),
        pltpu.SemaphoreType.DMA((2, LEVELS + 1)),
        pltpu.SemaphoreType.DMA((6,)),
        pltpu.SemaphoreType.DMA((2,)),
        pltpu.SemaphoreType.DMA((2,)),
        pltpu.SemaphoreType.DMA((2,)),
        pltpu.SemaphoreType.DMA((2,)),
        pltpu.SemaphoreType.DMA((2,)),
    ]
    results = pl.pallas_call(
        functools.partial(kernel, gx_size, gy_size, lvs + [wide]),
        out_shape=(
            jax.ShapeDtypeStruct(rhs.shape, jnp.float32),
            jax.ShapeDtypeStruct(rhs.shape, jnp.float32),
            jax.ShapeDtypeStruct(stencils.shape, jnp.float32),
        ),
        in_specs=[
            pl.BlockSpec(memory_space=pltpu.HBM),
            pl.BlockSpec(memory_space=pltpu.HBM),
            pl.BlockSpec(memory_space=pltpu.HBM),
            pl.BlockSpec(memory_space=pltpu.HBM),
        ],
        out_specs=(
            pl.BlockSpec(memory_space=pl.ANY),
            pl.BlockSpec(memory_space=pl.ANY),
            pl.BlockSpec(memory_space=pltpu.VMEM),
        ),
        scratch_shapes=scratch,
        compiler_params=pltpu.CompilerParams(
            collective_id=0, has_side_effects=True, vmem_limit_bytes=60 << 20
        ),
        cost_estimate=pl.CostEstimate(flops=60_000_000, bytes_accessed=1_100_000, transcendentals=0),
    )(rhs, target, stencils, face_mask)
    return pl.pallas_call(
        put_out,
        out_shape=tuple(jax.ShapeDtypeStruct(r.shape, r.dtype) for r in results),
        in_specs=[pl.BlockSpec(memory_space=pl.ANY)] * 3,
        out_specs=(pl.BlockSpec(memory_space=pl.ANY),) * 3,
        scratch_shapes=[pltpu.VMEM(r.shape, r.dtype) for r in results] + [pltpu.SemaphoreType.DMA((2, 3))],
        compiler_params=pltpu.CompilerParams(vmem_limit_bytes=60 << 20),
    )(*results)


def solution(mesh):
    sizes = dict(mesh.shape)
    return jax.shard_map(
        functools.partial(on_device, sizes["gx"], sizes["gy"]),
        mesh=mesh,
        in_specs=(P("gx", "gy", None), P("gx", "gy", None), P(), P()),
        out_specs=(P("gx", "gy", None), P("gx", "gy", None), P()),
        check_vma=False,
    )
```

```python
import functools

import jax
import jax.numpy as jnp
from jax import lax
from jax.experimental import pallas as pl
from jax.experimental.pallas import tpu as pltpu
from jax.sharding import PartitionSpec as P

MESH = pl.DeviceIdType.MESH
LEVELS = 4
NZ = 128
CHUNK = 384
UNROLL = 8
RIM = (3, 4, 5, 5, 7)
KNOWN = ((0, 0), (0, 0), (1, 0), (1, 1), (1, 1))
SCALES = tuple(4.0**level for level in range(LEVELS + 1))


def pieces(level, block, axis):
    rim = RIM[level]
    if level <= 1:
        return [(-1, block - rim, rim, False), (0, 0, block, False), (1, 0, rim, False)]
    if level == 2:
        if axis == 0:
            return [(-1, -1, 4, False), (0, -1, 6, False), (1, 1, 4, False)]
        return [(-1, 3, 5, False), (0, 0, 8, False), (1, 0, 5, False)]
    if level == 3:
        if axis == 0:
            return [(-2, -1, 4, True), (0, -1, 4, False), (2, -1, 4, True)]
        return [(-1, -1, 4, False), (0, -1, 6, False), (1, 1, 4, False)]
    if axis == 0:
        return [(d, -1, 3, d != 0) for d in (-6, -3, 0, 3, 6)]
    return [(-3, -1, 2, False), (-2, -1, 4, True), (0, -1, 4, False), (2, -1, 4, True), (3, 1, 2, False)]


class Level:
    def __init__(self, level, block):
        self.index = level
        self.rows, self.cols = block
        self.rim = RIM[level]
        self.high = self.rows + 2 * self.rim
        self.pitch = self.cols + 2 * self.rim
        self.store = self.high + 1
        while self.store * self.pitch % 8:
            self.store += 1
        known_rows, known_cols = KNOWN[level]
        self.pad_rows = known_rows + (self.rows if level >= 3 else 0)
        self.pad_cols = known_cols + (self.cols if level >= 4 else 0)
        self.stage_rows = self.rows + 2 * self.pad_rows
        self.stage_pitch = -(-(self.cols + 2 * self.pad_cols) // 8) * 8
        self.cuts = (pieces(level, self.rows, 0), pieces(level, self.cols, 1))
        received = sum(n for d, s, n, w in self.cuts[0]) * sum(n for d, s, n, w in self.cuts[1])
        own = [n for d, s, n, w in self.cuts[0] if d == 0][0] * [n for d, s, n, w in self.cuts[1] if d == 0][0]
        assert received == self.high * self.pitch
        self.arriving = received - own

    def span(self, depth):
        return depth * self.pitch + depth, (self.high - depth - 1) * self.pitch + self.pitch - depth


def blocks(first, last, body, chunk=CHUNK):
    count = last - first
    chunk = min(chunk, count)
    steps = -(-count // chunk)
    if steps <= 2:
        for step in range(steps):
            body(min(first + step * chunk, last - chunk), chunk)
        return

    def one(step, carry):
        body(jnp.minimum(first + step * chunk, last - chunk), chunk)
        return carry

    lax.fori_loop(0, steps, one, 0)


def hops_x(offset):
    return min(abs(offset), 8 - abs(offset)) + (offset != 0)


def hops_y(offset):
    return abs(offset) / 2


def lanes(shape):
    return lax.broadcasted_iota(jnp.int32, shape, 1)


def from_below(v):
    return jnp.where(lanes(v.shape) == 0, 0.0, pltpu.roll(v, 1, 1))


def from_above(v):
    return jnp.where(lanes(v.shape) == NZ - 1, 0.0, pltpu.roll(v, NZ - 1, 1))


def stencil_at(src, weight, pitch, row, rows):
    sums = [None, None, None]
    for a in range(3):
        for b in range(3):
            v = src[pl.ds(row + (a - 1) * pitch + b - 1, rows), :]
            for c in range(3):
                term = weight(9 * a + 3 * b + c) * v
                sums[c] = term if sums[c] is None else sums[c] + term
    return sums[1] + from_below(sums[0]) + from_above(sums[2])


def operate_at(src, diag, pitch, row, rows):
    v = src[pl.ds(row, rows), :]
    beside = (src[pl.ds(row - pitch, rows), :] + src[pl.ds(row + pitch, rows), :]) + (
        src[pl.ds(row - 1, rows), :] + src[pl.ds(row + 1, rows), :]
    )
    return diag[pl.ds(row, rows), :] * v - (beside + (from_below(v) + from_above(v)))


def smooth(dst, src, weight, lv, depth, mask=None, add=None):
    def body(row, rows):
        value = stencil_at(src, weight, lv.pitch, row, rows)
        if add is not None:
            value = value + add[pl.ds(row, rows), :]
        if mask is not None:
            value = value * mask[pl.ds(row, rows), :]
        dst[pl.ds(row, rows), :] = value

    blocks(*lv.span(depth), body)


def remain(dst, src, field, diag, mask, lv, depth):
    def body(row, rows):
        value = src[pl.ds(row, rows), :] - operate_at(field, diag, lv.pitch, row, rows)
        dst[pl.ds(row, rows), :] = value * mask[pl.ds(row, rows), :]

    blocks(*lv.span(depth), body)


def restrict(stage, fine, lv, below):
    known_rows, known_cols = KNOWN[below.index]
    first = -known_cols
    starts = range(first, below.cols + known_cols, 8)

    def body(step, carry):
        for start in starts:
            row = (lv.rim + 2 * (step - known_rows)) * lv.pitch + lv.rim + 2 * start
            total = (fine[pl.ds(row, 8, stride=2), :] + fine[pl.ds(row + 1, 8, stride=2), :]) + (
                fine[pl.ds(row + lv.pitch, 8, stride=2), :] + fine[pl.ds(row + lv.pitch + 1, 8, stride=2), :]
            )
            at = (below.pad_rows - known_rows + step) * below.stage_pitch + below.pad_cols + start
            width = min(8, below.cols + known_cols - start)
            stage[pl.ds(at, width), :] = 0.25 * total[:width]
        return carry

    count = below.rows + 2 * known_rows
    for step in range(count):
        body(step, 0)


def prolong_onto(dst, base, coarse, lv, below):
    half = 1 if lv.index == 0 else 2
    first, last = -half, below.cols + half
    starts = []
    start = first
    while True:
        if last - start <= 8:
            starts.append(max(first, last - 8))
            break
        starts.append(start)
        start += 8

    def body(step, carry):
        line = step - half
        values = [
            coarse[pl.ds((below.rim + line) * below.pitch + below.rim + start, 8), :] for start in starts
        ]
        for part in range(2):
            for start, value in zip(starts, values):
                row = (lv.rim + 2 * line + part) * lv.pitch + lv.rim + 2 * start
                for side in range(2):
                    where = pl.ds(row + side, 8, stride=2)
                    dst[where, :] = base[where, :] + value
        return carry

    for step in range(below.rows + 2 * half):
        body(step, 0)


def folded(v):
    rows = v.shape[0]
    total = v[0:8]
    for at in range(8, rows, 8):
        total = total + v[at : at + 8]
    return total


def products(cot, cot_first, cot_pitch, field, lv, totals=None):
    width = max(8, lv.cols)
    keep = None
    if lv.cols < 8:
        keep = lax.broadcasted_iota(jnp.int32, (8, NZ), 0) < lv.cols

    def body(step, totals):
        here = cot[pl.ds(cot_first + step * cot_pitch, width), :]
        if keep is not None:
            here = jnp.where(keep, here, 0.0)
        turned = (from_above(here), here, from_below(here))
        out = []
        for a in range(3):
            for b in range(3):
                v = field[pl.ds((lv.rim + step + a - 1) * lv.pitch + lv.rim + b - 1, width), :]
                for c in range(3):
                    out.append(totals[len(out)] + folded(turned[c] * v))
        return tuple(out)

    if totals is None:
        totals = tuple(jnp.zeros((8, NZ), jnp.float32) for _ in range(27))
    if lv.rows <= 2:
        for step in range(lv.rows):
            totals = body(step, totals)
        return totals
    unroll = min(UNROLL, lv.rows)

    def several(step, totals):
        for part in range(unroll):
            totals = body(step * unroll + part, totals)
        return totals

    return lax.fori_loop(0, lv.rows // unroll, several, totals)


def keep_sums(sums, totals, row):
    for entry, total in enumerate(totals):
        sums[pl.ds(row * 32 + entry, 1), :] = jnp.sum(total, axis=0, keepdims=True)


def kernel(gx_size, gy_size, lvs, rhs, target, stencils_in, walls_in, solution_out, grad_out, weights_out, *scratch):
    scratch = list(scratch)
    take = lambda: scratch.pop(0)
    src = [[take() for _ in lvs] for _ in range(2)]
    aft = [[take() for _ in lvs] for _ in range(2)]
    pre = [take() for _ in lvs]
    mid = [take() for _ in lvs]
    out = [take() for _ in lvs]
    mask = [take() for _ in lvs]
    diag = [take() for _ in lvs]
    stage = [take() for _ in lvs]
    last_rest = [take() for _ in range(2)]
    goal, result, grad, sums, mine, over_y, over_x = (take() for _ in range(7))
    stencils, walls = take(), take()
    recv, send, local, io, reduce_send, reduce_recv = (take() for _ in range(6))

    gx, gy = lax.axis_index("gx"), lax.axis_index("gy")

    def flat(ref, lv):
        return ref.reshape(2 * lv.stage_rows * lv.stage_pitch, NZ)

    stages = [flat(stage[i], lv) for i, lv in enumerate(lvs)]
    blocks3 = [[src[way][i].reshape(lv.store, lv.pitch, NZ) for i, lv in enumerate(lvs)] for way in range(2)]

    def device(x, y):
        return (lax.rem(x + 2 * gx_size, gx_size), lax.rem(y + 2 * gy_size, gy_size))

    barrier = pltpu.get_barrier_semaphore()
    near = [(d, e) for d in (-2, -1, 0, 1, 2) for e in (-1, 0, 1) if (d, e) != (0, 0)]
    near = sorted(set((d % gx_size, e % gy_size) for d, e in near))
    for d, e in near:
        pl.semaphore_signal(barrier, inc=1, device_id=device(gx + d, gy + e), device_id_type=MESH)

    load_rhs = pltpu.make_async_copy(rhs, stage[0].at[0], io.at[1])
    load_rhs.start()
    load_target = pltpu.make_async_copy(target, goal, io.at[0])
    load_target.start()
    load_walls = pltpu.make_async_copy(walls_in, walls, io.at[4])
    load_walls.start()
    load_stencils = pltpu.make_async_copy(stencils_in, stencils, io.at[5])
    load_stencils.start()
    for i, lv in enumerate(lvs):
        rows = lv.stage_rows * lv.stage_pitch
        first = rows if i < 2 else 0

        def clear(row, count, i=i):
            stages[i][pl.ds(row, count), :] = jnp.zeros((count, NZ), jnp.float32)

        blocks(first, 2 * rows, clear)

    def lay_out(i):
        lv = lvs[i]
        wall = [walls[k].astype(jnp.float32) for k in range(6)]
        total_rows, total_cols = gx_size * lv.rows, gy_size * lv.cols
        starts = list(range(0, lv.pitch, 8))

        def body(step, carry):
            line = gx * lv.rows - lv.rim + step
            first = jnp.where(line == 0, wall[0], 0.0) + jnp.where(line == total_rows - 1, wall[1], 0.0)
            within = (line >= 0) & (line < total_rows)
            for start in starts:
                column = gy * lv.cols - lv.rim + start + lax.broadcasted_iota(jnp.int32, (8, NZ), 0)
                lane = lanes((8, NZ))
                tally = first + jnp.where(column == 0, wall[2], 0.0) + jnp.where(column == total_cols - 1, wall[3], 0.0)
                tally = tally + jnp.where(lane == 0, wall[4], 0.0) + jnp.where(lane == NZ - 1, wall[5], 0.0)
                inside = (column >= 0) & (column < total_cols) & within
                where = pl.ds(step * lv.pitch + start, 8)
                diag[i][where, :] = 6.0 - tally
                mask[i][where, :] = jnp.where(inside, 1.0, 0.0)
            return carry

        lax.fori_loop(0, lv.high, body, 0)

    def placed(cut, me, size, block):
        offset, first, count, inward = cut
        if inward:
            low = offset > 0
            swapped = (me == 0) if low else (me == size - 1)
            step = -1 if low else 1
            acting = jnp.where(swapped, me + step, me)
            mirrored = jnp.where(swapped, -offset, offset)
            other = block - first - count
            begin = jnp.where(swapped, other + step * block, first)
            start = jnp.where(swapped, other, first)
        else:
            acting, mirrored, begin, start = me, offset, first, first
        to = acting - mirrored
        outside = (to < 0) | (to >= size)
        return begin, to, mirrored * block + start, outside, count

    def exchange(way, i):
        lv = lvs[i]
        across = [placed(cut, gx, gx_size, lv.rows) for cut in lv.cuts[0]]
        along = [placed(cut, gy, gy_size, lv.cols) for cut in lv.cuts[1]]
        pairs = [(p, q) for p in range(len(across)) for q in range(len(along))]
        pairs.sort(key=lambda pq: -(hops_x(lv.cuts[0][pq[0]][0]) + hops_y(lv.cuts[1][pq[1]][0])))
        for p, q in pairs:
            cut_x, cut_y = lv.cuts[0][p], lv.cuts[1][q]
            begin_x, to_x, land_x, out_x, count_x = across[p]
            begin_y, to_y, land_y, out_y, count_y = along[q]
            dst = blocks3[way][i].at[pl.ds(lv.rim + land_x, count_x), pl.ds(lv.rim + land_y, count_y)]
            if cut_x[0] == 0 and cut_y[0] == 0:
                piece = stage[i].at[
                    0, pl.ds(lv.pad_rows + begin_x, count_x), pl.ds(lv.pad_cols + begin_y, count_y)
                ]
                pltpu.make_async_copy(piece, dst, local.at[way, i]).start()
                continue
            piece = stage[i].at[
                jnp.where(out_x | out_y, 1, 0),
                pl.ds(lv.pad_rows + begin_x, count_x),
                pl.ds(lv.pad_cols + begin_y, count_y),
            ]
            pltpu.make_async_remote_copy(
                src_ref=piece,
                dst_ref=dst,
                send_sem=send.at[way, i],
                recv_sem=recv.at[way, i],
                device_id=device(to_x, to_y),
                device_id_type=MESH,
            ).start()

    def await_bytes(ref, rows, sem):
        pltpu.make_async_copy(ref.at[pl.ds(0, rows)], ref.at[pl.ds(0, rows)], sem).wait()

    def arrived(way, i):
        lv = lvs[i]
        await_bytes(src[way][i], lv.arriving, recv.at[way, i])
        await_bytes(src[way][i], lv.high * lv.pitch - lv.arriving, local.at[way, i])

    def sent(way, i):
        await_bytes(src[way][i], lvs[i].arriving, send.at[way, i])

    def weights(way, row):
        if way == 0:
            return lambda entry: stencils[row, entry]
        return lambda entry: stencils[row, 26 - entry]

    def cycle(way, waiting):
        for i in range(LEVELS):
            lv = lvs[i]
            exchange(way, i)
            waiting(i)
            arrived(way, i)
            smooth(pre[i], src[way][i], weights(way, i if way == 0 else LEVELS + i), lv, 1, mask[i])
            known = max(KNOWN[i + 1])
            remain(mid[i], src[way][i], pre[i], diag[i], mask[i], lv, lv.rim - 2 * known)
            sent(way, i)
            if way == 1 and i + 1 == LEVELS:
                sent(0, LEVELS)
            restrict(stages[i + 1], mid[i], lv, lvs[i + 1])
        bottom = lvs[LEVELS]
        weight = weights(way, 2 * LEVELS)
        exchange(way, LEVELS)
        waiting(LEVELS)
        arrived(way, LEVELS)
        b = src[way][LEVELS]
        x, y = pre[LEVELS], mid[LEVELS]
        rest = (aft[way][LEVELS], last_rest[way])
        smooth(x, b, weight, bottom, 1, mask[LEVELS])
        remain(rest[0], b, x, diag[LEVELS], mask[LEVELS], bottom, 2)
        smooth(y, rest[0], weight, bottom, 3, mask[LEVELS], x)
        remain(rest[1], b, y, diag[LEVELS], mask[LEVELS], bottom, 4)
        smooth(out[LEVELS], rest[1], weight, bottom, 5, mask[LEVELS], y)
        if way == 1:
            sent(1, LEVELS)
        for i in reversed(range(LEVELS)):
            lv = lvs[i]
            prolong_onto(mid[i], pre[i], out[i + 1], lv, lvs[i + 1])
            remain(aft[way][i], src[way][i], mid[i], diag[i], mask[i], lv, 2)
            if i > 0:
                smooth(out[i], aft[way][i], weights(way, LEVELS + i if way == 0 else i), lv, 3, mask[i], mid[i])

    def finish(weight, way, store):
        lv = lvs[0]

        def body(step, carry):
            for part in range(UNROLL):
                line = step * UNROLL + part
                row = (lv.rim + line) * lv.pitch + lv.rim
                value = stencil_at(aft[way][0], weight, lv.pitch, row, lv.cols)
                store(line, value + mid[0][pl.ds(row, lv.cols), :])
            return carry

        lax.fori_loop(0, lv.rows // UNROLL, body, 0)

    load_walls.wait()
    load_stencils.wait()
    load_rhs.wait()
    pl.semaphore_wait(barrier, len(near))

    def forward_waits(i):
        if i == 0:
            for level in range(LEVELS + 1):
                lay_out(level)
            rows = sums.shape[0]
            sums[...] = jnp.zeros((rows, NZ), jnp.float32)

    cycle(0, forward_waits)

    load_target.wait()

    def store_solution(step, value):
        result[step] = value
        stage[0][0, step] = value - goal[step]

    finish(weights(0, LEVELS), 0, store_solution)
    save_solution = pltpu.make_async_copy(result, solution_out, io.at[2])
    save_solution.start()

    def backward_waits(i):
        lv = lvs[i]
        if i < LEVELS:
            first = lv.pad_rows * lv.stage_pitch + lv.pad_cols
            keep_sums(sums, products(stages[i], first, lv.stage_pitch, aft[0][i], lv), LEVELS + i)

    cycle(1, backward_waits)

    bottom = lvs[LEVELS]
    at = bottom.rim * bottom.pitch + bottom.rim
    totals = products(src[1][LEVELS], at, bottom.pitch, last_rest[0], bottom)
    totals = products(aft[1][LEVELS], at, bottom.pitch, aft[0][LEVELS], bottom, totals)
    totals = products(last_rest[1], at, bottom.pitch, src[0][LEVELS], bottom, totals)
    keep_sums(sums, totals, 2 * LEVELS)
    for i in reversed(range(LEVELS)):
        lv = lvs[i]
        at = lv.rim * lv.pitch + lv.rim
        keep_sums(sums, products(aft[1][i], at, lv.pitch, src[0][i], lv), i)

    ones = jnp.ones((8, NZ), jnp.float32)
    for part in range(3):
        line = lax.dot_general(
            ones,
            sums[pl.ds(part * NZ, NZ), :],
            (((1,), (1,)), ((), ())),
            precision=lax.Precision.HIGHEST,
            preferred_element_type=jnp.float32,
        )
        mine[0, pl.ds(part, 1), :] = line[0:1]

    def spread(slot, held, me, order, where):
        source = mine.at[slot, pl.ds(0, 3)]
        for step in order:
            pltpu.make_async_remote_copy(
                src_ref=source,
                dst_ref=held.at[me, pl.ds(0, 3)],
                send_sem=reduce_send.at[slot],
                recv_sem=reduce_recv.at[slot],
                device_id=where(step),
                device_id_type=MESH,
            ).start()
        held[me] = mine[slot]

    def gathered(slot, held, size):
        await_bytes(src[0][0], 3 * (size - 1), reduce_recv.at[slot])
        total = held[0]
        for step in range(1, size):
            total = total + held[step]
        return total

    order = sorted(range(1, gy_size), key=lambda step: -min(step, gy_size - step))
    spread(0, over_y, gy, order, lambda step: device(gx, gy + step))

    def store_grad(step, value):
        grad[step] = value

    finish(weights(1, 0), 1, store_grad)
    save_grad = pltpu.make_async_copy(grad, grad_out, io.at[3])
    save_grad.start()

    mine[1] = gathered(0, over_y, gy_size)
    order = sorted(range(1, gx_size), key=lambda step: -min(step % 8, 8 - step % 8) - min(step, gx_size - step) / 8)
    spread(1, over_x, gx, order, lambda step: device(gx + step, gy))
    await_bytes(src[0][0], 3 * (gy_size - 1), reduce_send.at[0])
    save_solution.wait()
    save_grad.wait()
    total = gathered(1, over_x, gx_size)
    await_bytes(src[0][0], 3 * (gx_size - 1), reduce_send.at[1])
    cells = gx_size * lvs[0].rows * gy_size * lvs[0].cols * NZ
    for row in range(2 * LEVELS + 1):
        scale = SCALES[row % LEVELS if row < 2 * LEVELS else LEVELS] / cells
        part, lane = row // 4, 32 * (row % 4)
        weights_out[pl.ds(row, 1), :] = total[part : part + 1, lane : lane + 27] * scale


def put_out(*refs):
    sources, targets, held, sems = refs[:3], refs[3:6], refs[6:9], refs[9]
    loads = [pltpu.make_async_copy(sources[i], held[i], sems.at[0, i]) for i in range(3)]
    stores = [pltpu.make_async_copy(held[i], targets[i], sems.at[1, i]) for i in range(3)]
    for load in loads:
        load.start()
    for load, store in zip(loads, stores):
        load.wait()
        store.start()
    for store in stores:
        store.wait()


def on_device(gx_size, gy_size, rhs, target, stencils, face_mask):
    rows, cols, _ = rhs.shape
    lvs = [Level(i, (rows >> i, cols >> i)) for i in range(LEVELS + 1)]
    field = lambda lv: pltpu.VMEM((lv.store * lv.pitch, NZ), jnp.float32)
    scratch = []
    for _ in range(9):
        scratch += [field(lv) for lv in lvs]
    scratch += [pltpu.VMEM((2, lv.stage_rows, lv.stage_pitch, NZ), jnp.float32) for lv in lvs]
    scratch += [field(lvs[LEVELS])] * 2
    scratch += [pltpu.VMEM((rows, cols, NZ), jnp.float32)] * 3
    scratch += [
        pltpu.VMEM((3 * NZ, NZ), jnp.float32),
        pltpu.VMEM((2, 8, NZ), jnp.float32),
        pltpu.VMEM((gy_size, 8, NZ), jnp.float32),
        pltpu.VMEM((gx_size, 8, NZ), jnp.float32),
        pltpu.SMEM(stencils.shape, jnp.float32),
        pltpu.SMEM(face_mask.shape, jnp.int32),
        pltpu.SemaphoreType.DMA((2, LEVELS + 1)),
        pltpu.SemaphoreType.DMA((2, LEVELS + 1)),
        pltpu.SemaphoreType.DMA((2, LEVELS + 1)),
        pltpu.SemaphoreType.DMA((6,)),
        pltpu.SemaphoreType.DMA((2,)),
        pltpu.SemaphoreType.DMA((2,)),
    ]
    results = pl.pallas_call(
        functools.partial(kernel, gx_size, gy_size, lvs),
        out_shape=(
            jax.ShapeDtypeStruct(rhs.shape, jnp.float32),
            jax.ShapeDtypeStruct(rhs.shape, jnp.float32),
            jax.ShapeDtypeStruct(stencils.shape, jnp.float32),
        ),
        in_specs=[
            pl.BlockSpec(memory_space=pltpu.HBM),
            pl.BlockSpec(memory_space=pltpu.HBM),
            pl.BlockSpec(memory_space=pltpu.HBM),
            pl.BlockSpec(memory_space=pltpu.HBM),
        ],
        out_specs=(
            pl.BlockSpec(memory_space=pl.ANY),
            pl.BlockSpec(memory_space=pl.ANY),
            pl.BlockSpec(memory_space=pltpu.VMEM),
        ),
        scratch_shapes=scratch,
        compiler_params=pltpu.CompilerParams(
            collective_id=0, has_side_effects=True, vmem_limit_bytes=60 << 20
        ),
        cost_estimate=pl.CostEstimate(flops=60_000_000, bytes_accessed=1_100_000, transcendentals=0),
    )(rhs, target, stencils, face_mask)
    return pl.pallas_call(
        put_out,
        out_shape=tuple(jax.ShapeDtypeStruct(r.shape, r.dtype) for r in results),
        in_specs=[pl.BlockSpec(memory_space=pl.ANY)] * 3,
        out_specs=(pl.BlockSpec(memory_space=pl.ANY),) * 3,
        scratch_shapes=[pltpu.VMEM(r.shape, r.dtype) for r in results] + [pltpu.SemaphoreType.DMA((2, 3))],
        compiler_params=pltpu.CompilerParams(vmem_limit_bytes=60 << 20),
    )(*results)


def solution(mesh):
    sizes = dict(mesh.shape)
    return jax.shard_map(
        functools.partial(on_device, sizes["gx"], sizes["gy"]),
        mesh=mesh,
        in_specs=(P("gx", "gy", None), P("gx", "gy", None), P(), P()),
        out_specs=(P("gx", "gy", None), P("gx", "gy", None), P()),
        check_vma=False,
    )
```

```python
import functools

import jax
import jax.numpy as jnp
from jax import lax
from jax.experimental import pallas as pl
from jax.experimental.pallas import tpu as pltpu
from jax.sharding import PartitionSpec as P

MESH = pl.DeviceIdType.MESH
LEVELS = 4
NZ = 128
CHUNK = 1024
UNROLL = 8
RIM = (3, 4, 5, 5, 7)
KNOWN = ((0, 0), (0, 0), (1, 0), (1, 1), (1, 1))
SCALES = tuple(4.0**level for level in range(LEVELS + 1))


def pieces(level, block, axis):
    rim = RIM[level]
    if level <= 1:
        return [(-1, block - rim, rim, False), (0, 0, block, False), (1, 0, rim, False)]
    if level == 2:
        if axis == 0:
            return [(-1, -1, 4, False), (0, -1, 6, False), (1, 1, 4, False)]
        return [(-1, 3, 5, False), (0, 0, 8, False), (1, 0, 5, False)]
    if level == 3:
        if axis == 0:
            return [(-2, -1, 4, True), (0, -1, 4, False), (2, -1, 4, True)]
        return [(-1, -1, 4, False), (0, -1, 6, False), (1, 1, 4, False)]
    if axis == 0:
        return [(d, -1, 3, d != 0) for d in (-6, -3, 0, 3, 6)]
    return [(-3, -1, 2, False), (-2, -1, 4, True), (0, -1, 4, False), (2, -1, 4, True), (3, 1, 2, False)]


class Level:
    def __init__(self, level, block):
        self.index = level
        self.rows, self.cols = block
        self.rim = RIM[level]
        self.high = self.rows + 2 * self.rim
        self.pitch = self.cols + 2 * self.rim
        self.store = self.high + 1
        while self.store * self.pitch % 8:
            self.store += 1
        known_rows, known_cols = KNOWN[level]
        self.pad_rows = known_rows + (self.rows if level >= 3 else 0)
        self.pad_cols = known_cols + (self.cols if level >= 4 else 0)
        self.stage_rows = self.rows + 2 * self.pad_rows
        self.stage_pitch = -(-(self.cols + 2 * self.pad_cols) // 8) * 8
        self.cuts = (pieces(level, self.rows, 0), pieces(level, self.cols, 1))
        received = sum(n for d, s, n, w in self.cuts[0]) * sum(n for d, s, n, w in self.cuts[1])
        own = [n for d, s, n, w in self.cuts[0] if d == 0][0] * [n for d, s, n, w in self.cuts[1] if d == 0][0]
        assert received == self.high * self.pitch
        self.arriving = received - own

    def span(self, depth):
        return depth * self.pitch + depth, (self.high - depth - 1) * self.pitch + self.pitch - depth


def blocks(first, last, body, chunk=CHUNK):
    count = last - first
    chunk = min(chunk, count)
    steps = -(-count // chunk)
    if steps <= 2:
        for step in range(steps):
            body(min(first + step * chunk, last - chunk), chunk)
        return

    def one(step, carry):
        body(jnp.minimum(first + step * chunk, last - chunk), chunk)
        return carry

    lax.fori_loop(0, steps, one, 0)


def hops_x(offset):
    return min(abs(offset), 8 - abs(offset)) + (offset != 0)


def hops_y(offset):
    return abs(offset) / 2


def lanes(shape):
    return lax.broadcasted_iota(jnp.int32, shape, 1)


def from_below(v):
    return jnp.where(lanes(v.shape) == 0, 0.0, pltpu.roll(v, 1, 1))


def from_above(v):
    return jnp.where(lanes(v.shape) == NZ - 1, 0.0, pltpu.roll(v, NZ - 1, 1))


def stencil_at(src, weight, pitch, row, rows):
    sums = [None, None, None]
    for a in range(3):
        for b in range(3):
            v = src[pl.ds(row + (a - 1) * pitch + b - 1, rows), :]
            for c in range(3):
                term = weight(9 * a + 3 * b + c) * v
                sums[c] = term if sums[c] is None else sums[c] + term
    return sums[1] + from_below(sums[0]) + from_above(sums[2])


def operate_at(src, diag, pitch, row, rows):
    v = src[pl.ds(row, rows), :]
    beside = (src[pl.ds(row - pitch, rows), :] + src[pl.ds(row + pitch, rows), :]) + (
        src[pl.ds(row - 1, rows), :] + src[pl.ds(row + 1, rows), :]
    )
    return diag[pl.ds(row, rows), :] * v - (beside + (from_below(v) + from_above(v)))


def smooth(dst, src, weight, lv, depth, mask=None, add=None):
    def body(row, rows):
        value = stencil_at(src, weight, lv.pitch, row, rows)
        if add is not None:
            value = value + add[pl.ds(row, rows), :]
        if mask is not None:
            value = value * mask[pl.ds(row, rows), :]
        dst[pl.ds(row, rows), :] = value

    blocks(*lv.span(depth), body)


def remain(dst, src, field, diag, mask, lv, depth):
    def body(row, rows):
        value = src[pl.ds(row, rows), :] - operate_at(field, diag, lv.pitch, row, rows)
        dst[pl.ds(row, rows), :] = value * mask[pl.ds(row, rows), :]

    blocks(*lv.span(depth), body)


def restrict(stage, fine, lv, below):
    known_rows, known_cols = KNOWN[below.index]
    first = -known_cols
    starts = range(first, below.cols + known_cols, 8)

    def body(step, carry):
        for start in starts:
            row = (lv.rim + 2 * (step - known_rows)) * lv.pitch + lv.rim + 2 * start
            total = (fine[pl.ds(row, 8, stride=2), :] + fine[pl.ds(row + 1, 8, stride=2), :]) + (
                fine[pl.ds(row + lv.pitch, 8, stride=2), :] + fine[pl.ds(row + lv.pitch + 1, 8, stride=2), :]
            )
            at = (below.pad_rows - known_rows + step) * below.stage_pitch + below.pad_cols + start
            width = min(8, below.cols + known_cols - start)
            stage[pl.ds(at, width), :] = 0.25 * total[:width]
        return carry

    count = below.rows + 2 * known_rows
    for step in range(count):
        body(step, 0)


def prolong_onto(dst, base, coarse, lv, below):
    half = 1 if lv.index == 0 else 2
    first, last = -half, below.cols + half
    starts = []
    start = first
    while True:
        if last - start <= 8:
            starts.append(max(first, last - 8))
            break
        starts.append(start)
        start += 8

    def body(step, carry):
        line = step - half
        values = [
            coarse[pl.ds((below.rim + line) * below.pitch + below.rim + start, 8), :] for start in starts
        ]
        for part in range(2):
            for start, value in zip(starts, values):
                row = (lv.rim + 2 * line + part) * lv.pitch + lv.rim + 2 * start
                for side in range(2):
                    where = pl.ds(row + side, 8, stride=2)
                    dst[where, :] = base[where, :] + value
        return carry

    for step in range(below.rows + 2 * half):
        body(step, 0)


def folded(v):
    rows = v.shape[0]
    total = v[0:8]
    for at in range(8, rows, 8):
        total = total + v[at : at + 8]
    return total


def products(cot, cot_first, cot_pitch, field, lv, totals=None):
    width = max(8, lv.cols)
    keep = None
    if lv.cols < 8:
        keep = lax.broadcasted_iota(jnp.int32, (8, NZ), 0) < lv.cols

    def body(step, totals):
        here = cot[pl.ds(cot_first + step * cot_pitch, width), :]
        if keep is not None:
            here = jnp.where(keep, here, 0.0)
        turned = (from_above(here), here, from_below(here))
        out = []
        for a in range(3):
            for b in range(3):
                v = field[pl.ds((lv.rim + step + a - 1) * lv.pitch + lv.rim + b - 1, width), :]
                for c in range(3):
                    out.append(totals[len(out)] + folded(turned[c] * v))
        return tuple(out)

    if totals is None:
        totals = tuple(jnp.zeros((8, NZ), jnp.float32) for _ in range(27))
    if lv.rows <= 2:
        for step in range(lv.rows):
            totals = body(step, totals)
        return totals
    unroll = min(UNROLL, lv.rows)

    def several(step, totals):
        for part in range(unroll):
            totals = body(step * unroll + part, totals)
        return totals

    return lax.fori_loop(0, lv.rows // unroll, several, totals)


def keep_sums(sums, totals, row):
    for entry, total in enumerate(totals):
        sums[pl.ds(row * 32 + entry, 1), :] = jnp.sum(total, axis=0, keepdims=True)


def kernel(gx_size, gy_size, lvs, rhs, target, stencils_in, walls_in, solution_out, grad_out, weights_out, *scratch):
    scratch = list(scratch)
    take = lambda: scratch.pop(0)
    src = [[take() for _ in lvs] for _ in range(2)]
    aft = [[take() for _ in lvs] for _ in range(2)]
    pre = [take() for _ in lvs]
    mid = [take() for _ in lvs]
    out = [take() for _ in lvs]
    mask = [take() for _ in lvs]
    diag = [take() for _ in lvs]
    stage = [take() for _ in lvs]
    last_rest = [take() for _ in range(2)]
    goal, result, grad, sums, mine, over_y, over_x = (take() for _ in range(7))
    stencils, walls = take(), take()
    recv, send, local, io, reduce_send, reduce_recv = (take() for _ in range(6))

    gx, gy = lax.axis_index("gx"), lax.axis_index("gy")

    def flat(ref, lv):
        return ref.reshape(2 * lv.stage_rows * lv.stage_pitch, NZ)

    stages = [flat(stage[i], lv) for i, lv in enumerate(lvs)]
    blocks3 = [[src[way][i].reshape(lv.store, lv.pitch, NZ) for i, lv in enumerate(lvs)] for way in range(2)]

    def device(x, y):
        return (lax.rem(x + 2 * gx_size, gx_size), lax.rem(y + 2 * gy_size, gy_size))

    barrier = pltpu.get_barrier_semaphore()
    near = [(d, e) for d in (-2, -1, 0, 1, 2) for e in (-1, 0, 1) if (d, e) != (0, 0)]
    near = sorted(set((d % gx_size, e % gy_size) for d, e in near))
    for d, e in near:
        pl.semaphore_signal(barrier, inc=1, device_id=device(gx + d, gy + e), device_id_type=MESH)

    load_rhs = pltpu.make_async_copy(rhs, stage[0].at[0], io.at[1])
    load_rhs.start()
    load_target = pltpu.make_async_copy(target, goal, io.at[0])
    load_target.start()
    load_walls = pltpu.make_async_copy(walls_in, walls, io.at[4])
    load_walls.start()
    load_stencils = pltpu.make_async_copy(stencils_in, stencils, io.at[5])
    load_stencils.start()
    for i, lv in enumerate(lvs):
        rows = lv.stage_rows * lv.stage_pitch
        first = rows if i < 2 else 0

        def clear(row, count, i=i):
            stages[i][pl.ds(row, count), :] = jnp.zeros((count, NZ), jnp.float32)

        blocks(first, 2 * rows, clear)

    def lay_out(i):
        lv = lvs[i]
        wall = [walls[k].astype(jnp.float32) for k in range(6)]
        total_rows, total_cols = gx_size * lv.rows, gy_size * lv.cols
        starts = list(range(0, lv.pitch, 8))

        def body(step, carry):
            line = gx * lv.rows - lv.rim + step
            first = jnp.where(line == 0, wall[0], 0.0) + jnp.where(line == total_rows - 1, wall[1], 0.0)
            within = (line >= 0) & (line < total_rows)
            for start in starts:
                column = gy * lv.cols - lv.rim + start + lax.broadcasted_iota(jnp.int32, (8, NZ), 0)
                lane = lanes((8, NZ))
                tally = first + jnp.where(column == 0, wall[2], 0.0) + jnp.where(column == total_cols - 1, wall[3], 0.0)
                tally = tally + jnp.where(lane == 0, wall[4], 0.0) + jnp.where(lane == NZ - 1, wall[5], 0.0)
                inside = (column >= 0) & (column < total_cols) & within
                where = pl.ds(step * lv.pitch + start, 8)
                diag[i][where, :] = 6.0 - tally
                mask[i][where, :] = jnp.where(inside, 1.0, 0.0)
            return carry

        lax.fori_loop(0, lv.high, body, 0)

    def placed(cut, me, size, block):
        offset, first, count, inward = cut
        if inward:
            low = offset > 0
            swapped = (me == 0) if low else (me == size - 1)
            step = -1 if low else 1
            acting = jnp.where(swapped, me + step, me)
            mirrored = jnp.where(swapped, -offset, offset)
            other = block - first - count
            begin = jnp.where(swapped, other + step * block, first)
            start = jnp.where(swapped, other, first)
        else:
            acting, mirrored, begin, start = me, offset, first, first
        to = acting - mirrored
        outside = (to < 0) | (to >= size)
        return begin, to, mirrored * block + start, outside, count

    def exchange(way, i):
        lv = lvs[i]
        across = [placed(cut, gx, gx_size, lv.rows) for cut in lv.cuts[0]]
        along = [placed(cut, gy, gy_size, lv.cols) for cut in lv.cuts[1]]
        pairs = [(p, q) for p in range(len(across)) for q in range(len(along))]
        pairs.sort(key=lambda pq: -(hops_x(lv.cuts[0][pq[0]][0]) + hops_y(lv.cuts[1][pq[1]][0])))
        for p, q in pairs:
            cut_x, cut_y = lv.cuts[0][p], lv.cuts[1][q]
            begin_x, to_x, land_x, out_x, count_x = across[p]
            begin_y, to_y, land_y, out_y, count_y = along[q]
            dst = blocks3[way][i].at[pl.ds(lv.rim + land_x, count_x), pl.ds(lv.rim + land_y, count_y)]
            if cut_x[0] == 0 and cut_y[0] == 0:
                piece = stage[i].at[
                    0, pl.ds(lv.pad_rows + begin_x, count_x), pl.ds(lv.pad_cols + begin_y, count_y)
                ]
                pltpu.make_async_copy(piece, dst, local.at[way, i]).start()
                continue
            piece = stage[i].at[
                jnp.where(out_x | out_y, 1, 0),
                pl.ds(lv.pad_rows + begin_x, count_x),
                pl.ds(lv.pad_cols + begin_y, count_y),
            ]
            pltpu.make_async_remote_copy(
                src_ref=piece,
                dst_ref=dst,
                send_sem=send.at[way, i],
                recv_sem=recv.at[way, i],
                device_id=device(to_x, to_y),
                device_id_type=MESH,
            ).start()

    def await_bytes(ref, rows, sem):
        pltpu.make_async_copy(ref.at[pl.ds(0, rows)], ref.at[pl.ds(0, rows)], sem).wait()

    def arrived(way, i):
        lv = lvs[i]
        await_bytes(src[way][i], lv.arriving, recv.at[way, i])
        await_bytes(src[way][i], lv.high * lv.pitch - lv.arriving, local.at[way, i])

    def sent(way, i):
        await_bytes(src[way][i], lvs[i].arriving, send.at[way, i])

    def weights(way, row):
        if way == 0:
            return lambda entry: stencils[row, entry]
        return lambda entry: stencils[row, 26 - entry]

    def cycle(way, waiting):
        for i in range(LEVELS):
            lv = lvs[i]
            exchange(way, i)
            waiting(i)
            arrived(way, i)
            smooth(pre[i], src[way][i], weights(way, i if way == 0 else LEVELS + i), lv, 1, mask[i])
            known = max(KNOWN[i + 1])
            remain(mid[i], src[way][i], pre[i], diag[i], mask[i], lv, lv.rim - 2 * known)
            sent(way, i)
            if way == 1 and i + 1 == LEVELS:
                sent(0, LEVELS)
            restrict(stages[i + 1], mid[i], lv, lvs[i + 1])
        bottom = lvs[LEVELS]
        weight = weights(way, 2 * LEVELS)
        exchange(way, LEVELS)
        waiting(LEVELS)
        arrived(way, LEVELS)
        b = src[way][LEVELS]
        x, y = pre[LEVELS], mid[LEVELS]
        rest = (aft[way][LEVELS], last_rest[way])
        smooth(x, b, weight, bottom, 1, mask[LEVELS])
        remain(rest[0], b, x, diag[LEVELS], mask[LEVELS], bottom, 2)
        smooth(y, rest[0], weight, bottom, 3, mask[LEVELS], x)
        remain(rest[1], b, y, diag[LEVELS], mask[LEVELS], bottom, 4)
        smooth(out[LEVELS], rest[1], weight, bottom, 5, mask[LEVELS], y)
        if way == 1:
            sent(1, LEVELS)
        for i in reversed(range(LEVELS)):
            lv = lvs[i]
            prolong_onto(mid[i], pre[i], out[i + 1], lv, lvs[i + 1])
            remain(aft[way][i], src[way][i], mid[i], diag[i], mask[i], lv, 2)
            if i > 0:
                smooth(out[i], aft[way][i], weights(way, LEVELS + i if way == 0 else i), lv, 3, mask[i], mid[i])

    def finish(weight, way, store):
        lv = lvs[0]

        def body(step, carry):
            for part in range(UNROLL):
                line = step * UNROLL + part
                row = (lv.rim + line) * lv.pitch + lv.rim
                value = stencil_at(aft[way][0], weight, lv.pitch, row, lv.cols)
                store(line, value + mid[0][pl.ds(row, lv.cols), :])
            return carry

        lax.fori_loop(0, lv.rows // UNROLL, body, 0)

    load_walls.wait()
    load_stencils.wait()
    load_rhs.wait()
    pl.semaphore_wait(barrier, len(near))

    def forward_waits(i):
        if i == 0:
            for level in range(LEVELS + 1):
                lay_out(level)
            rows = sums.shape[0]
            sums[...] = jnp.zeros((rows, NZ), jnp.float32)

    cycle(0, forward_waits)

    load_target.wait()

    def store_solution(step, value):
        result[step] = value
        stage[0][0, step] = value - goal[step]

    finish(weights(0, LEVELS), 0, store_solution)
    save_solution = pltpu.make_async_copy(result, solution_out, io.at[2])
    save_solution.start()

    def backward_waits(i):
        lv = lvs[i]
        if i < LEVELS:
            first = lv.pad_rows * lv.stage_pitch + lv.pad_cols
            keep_sums(sums, products(stages[i], first, lv.stage_pitch, aft[0][i], lv), LEVELS + i)

    cycle(1, backward_waits)

    bottom = lvs[LEVELS]
    at = bottom.rim * bottom.pitch + bottom.rim
    totals = products(src[1][LEVELS], at, bottom.pitch, last_rest[0], bottom)
    totals = products(aft[1][LEVELS], at, bottom.pitch, aft[0][LEVELS], bottom, totals)
    totals = products(last_rest[1], at, bottom.pitch, src[0][LEVELS], bottom, totals)
    keep_sums(sums, totals, 2 * LEVELS)
    for i in reversed(range(LEVELS)):
        lv = lvs[i]
        at = lv.rim * lv.pitch + lv.rim
        keep_sums(sums, products(aft[1][i], at, lv.pitch, src[0][i], lv), i)

    ones = jnp.ones((8, NZ), jnp.float32)
    for part in range(3):
        line = lax.dot_general(
            ones,
            sums[pl.ds(part * NZ, NZ), :],
            (((1,), (1,)), ((), ())),
            precision=lax.Precision.HIGHEST,
            preferred_element_type=jnp.float32,
        )
        mine[0, pl.ds(part, 1), :] = line[0:1]

    def spread(slot, held, me, order, where):
        source = mine.at[slot, pl.ds(0, 3)]
        for step in order:
            pltpu.make_async_remote_copy(
                src_ref=source,
                dst_ref=held.at[me, pl.ds(0, 3)],
                send_sem=reduce_send.at[slot],
                recv_sem=reduce_recv.at[slot],
                device_id=where(step),
                device_id_type=MESH,
            ).start()
        held[me] = mine[slot]

    def gathered(slot, held, size):
        await_bytes(src[0][0], 3 * (size - 1), reduce_recv.at[slot])
        total = held[0]
        for step in range(1, size):
            total = total + held[step]
        return total

    order = sorted(range(1, gy_size), key=lambda step: -min(step, gy_size - step))
    spread(0, over_y, gy, order, lambda step: device(gx, gy + step))

    def store_grad(step, value):
        grad[step] = value

    finish(weights(1, 0), 1, store_grad)
    save_grad = pltpu.make_async_copy(grad, grad_out, io.at[3])
    save_grad.start()

    mine[1] = gathered(0, over_y, gy_size)
    order = sorted(range(1, gx_size), key=lambda step: -min(step % 8, 8 - step % 8) - min(step, gx_size - step) / 8)
    spread(1, over_x, gx, order, lambda step: device(gx + step, gy))
    await_bytes(src[0][0], 3 * (gy_size - 1), reduce_send.at[0])
    save_solution.wait()
    save_grad.wait()
    total = gathered(1, over_x, gx_size)
    await_bytes(src[0][0], 3 * (gx_size - 1), reduce_send.at[1])
    cells = gx_size * lvs[0].rows * gy_size * lvs[0].cols * NZ
    for row in range(2 * LEVELS + 1):
        scale = SCALES[row % LEVELS if row < 2 * LEVELS else LEVELS] / cells
        part, lane = row // 4, 32 * (row % 4)
        weights_out[pl.ds(row, 1), :] = total[part : part + 1, lane : lane + 27] * scale


def put_out(*refs):
    sources, targets, held, sems = refs[:3], refs[3:6], refs[6:9], refs[9]
    loads = [pltpu.make_async_copy(sources[i], held[i], sems.at[0, i]) for i in range(3)]
    stores = [pltpu.make_async_copy(held[i], targets[i], sems.at[1, i]) for i in range(3)]
    for load in loads:
        load.start()
    for load, store in zip(loads, stores):
        load.wait()
        store.start()
    for store in stores:
        store.wait()


def on_device(gx_size, gy_size, rhs, target, stencils, face_mask):
    rows, cols, _ = rhs.shape
    lvs = [Level(i, (rows >> i, cols >> i)) for i in range(LEVELS + 1)]
    field = lambda lv: pltpu.VMEM((lv.store * lv.pitch, NZ), jnp.float32)
    scratch = []
    for _ in range(9):
        scratch += [field(lv) for lv in lvs]
    scratch += [pltpu.VMEM((2, lv.stage_rows, lv.stage_pitch, NZ), jnp.float32) for lv in lvs]
    scratch += [field(lvs[LEVELS])] * 2
    scratch += [pltpu.VMEM((rows, cols, NZ), jnp.float32)] * 3
    scratch += [
        pltpu.VMEM((3 * NZ, NZ), jnp.float32),
        pltpu.VMEM((2, 8, NZ), jnp.float32),
        pltpu.VMEM((gy_size, 8, NZ), jnp.float32),
        pltpu.VMEM((gx_size, 8, NZ), jnp.float32),
        pltpu.SMEM(stencils.shape, jnp.float32),
        pltpu.SMEM(face_mask.shape, jnp.int32),
        pltpu.SemaphoreType.DMA((2, LEVELS + 1)),
        pltpu.SemaphoreType.DMA((2, LEVELS + 1)),
        pltpu.SemaphoreType.DMA((2, LEVELS + 1)),
        pltpu.SemaphoreType.DMA((6,)),
        pltpu.SemaphoreType.DMA((2,)),
        pltpu.SemaphoreType.DMA((2,)),
    ]
    results = pl.pallas_call(
        functools.partial(kernel, gx_size, gy_size, lvs),
        out_shape=(
            jax.ShapeDtypeStruct(rhs.shape, jnp.float32),
            jax.ShapeDtypeStruct(rhs.shape, jnp.float32),
            jax.ShapeDtypeStruct(stencils.shape, jnp.float32),
        ),
        in_specs=[
            pl.BlockSpec(memory_space=pltpu.HBM),
            pl.BlockSpec(memory_space=pltpu.HBM),
            pl.BlockSpec(memory_space=pltpu.HBM),
            pl.BlockSpec(memory_space=pltpu.HBM),
        ],
        out_specs=(
            pl.BlockSpec(memory_space=pl.ANY),
            pl.BlockSpec(memory_space=pl.ANY),
            pl.BlockSpec(memory_space=pltpu.VMEM),
        ),
        scratch_shapes=scratch,
        compiler_params=pltpu.CompilerParams(
            collective_id=0, has_side_effects=True, vmem_limit_bytes=60 << 20
        ),
        cost_estimate=pl.CostEstimate(flops=60_000_000, bytes_accessed=1_100_000, transcendentals=0),
    )(rhs, target, stencils, face_mask)
    return pl.pallas_call(
        put_out,
        out_shape=tuple(jax.ShapeDtypeStruct(r.shape, r.dtype) for r in results),
        in_specs=[pl.BlockSpec(memory_space=pl.ANY)] * 3,
        out_specs=(pl.BlockSpec(memory_space=pl.ANY),) * 3,
        scratch_shapes=[pltpu.VMEM(r.shape, r.dtype) for r in results] + [pltpu.SemaphoreType.DMA((2, 3))],
        compiler_params=pltpu.CompilerParams(vmem_limit_bytes=60 << 20),
    )(*results)


def solution(mesh):
    sizes = dict(mesh.shape)
    return jax.shard_map(
        functools.partial(on_device, sizes["gx"], sizes["gy"]),
        mesh=mesh,
        in_specs=(P("gx", "gy", None), P("gx", "gy", None), P(), P()),
        out_specs=(P("gx", "gy", None), P("gx", "gy", None), P()),
        check_vma=False,
    )
```
